128 devices in a mesh: blk: 16 (over z, y_lo, core), dp: 8 (over y_hi, x).
Axes of the slice: x: 4, y: 4 (y_hi: 2, y_lo: 2; y = y_hi * 2 + y_lo), z: 4, core: 2. Of those that a mesh axis runs over, the one named last changes fastest.
Arguments:
- pooled_image_rows: bfloat16 [8, 6144, 1152], P('dp', 'blk'), may hold values from -6 to 6
- text_embed_rows: bfloat16 [8, 6144, 1152], P('dp', 'blk'), may hold values from -6 to 6
- projection_matrix: bfloat16 [1152, 1152], replicated, may hold values from -0.1875 to 0.1875
- lowrank_down_weight: bfloat16 [1152, 64], replicated, may hold values from -0.1875 to 0.1875
- lowrank_up_weight: bfloat16 [64, 1152], replicated, may hold values from -0.75 to 0.75
- similarity_scale: float32 [1], replicated, may hold values from 2 to 5
- similarity_bias: float32 [1], replicated, may hold values from -6 to -2
Outputs:
- text_grad: float32 [8, 6144, 1152], P('dp', 'blk')
- grad_down: float32 [1152, 64], replicated
- grad_up: float32 [64, 1152], replicated
The draws below stay inside these ranges and needn't reach their ends.
All inputs are finite; a program needn't handle non-finite values.
Results may differ from the reference program's by a relative error of at most 0.0015.
Values may be sent and summed in bfloat16 or wider, within the bound.
No kernel may reach another device: no remote copies, remote signals or barrier semaphores. Data moves between devices by JAX's collectives and lax.ppermute only.
A program may use at most 128 MiB of HBM per device.

```python
import math
import jax
import jax.numpy as jnp
from jax import lax

POOLED_WIDTH = 1152
EMBED_WIDTH = 1152
ADAPTER_RANK = 64
PAIRS = 6144
N_DP = 8


def block_scale(stream_key, dims, pieces, least, largest):
    gain, own = 1.0, jax.random.fold_in(stream_key, 6)
    for dim, shards_of in pieces:
        heights = jnp.exp(jax.random.uniform(jax.random.fold_in(own, dim), (shards_of,), jnp.float32, least / len(pieces), largest / len(pieces)))
        gain = gain * jnp.repeat(heights, dims[dim] // shards_of).reshape([-1 if axis == dim else 1 for axis in range(len(dims))])
    return gain


def normal_values(rng, shape, deviation, reach, split=(), kind=jnp.bfloat16):
    loudness = block_scale(rng, shape, split, -0.22, 0.18) if split else 1.0
    result = jax.random.normal(rng, shape, jnp.float32) * deviation * loudness
    return jnp.minimum(jnp.maximum(result, -reach), reach).astype(kind)


def setup_inputs(seed: int = 0) -> dict:
    key_of = jax.random.split(jax.random.key(seed), 8)
    pooled_image_rows = normal_values(key_of[0], (N_DP, PAIRS, POOLED_WIDTH), 1.0, 6.0, ((0, 8), (1, 16)))
    text_embed_rows = normal_values(key_of[1], (N_DP, PAIRS, EMBED_WIDTH), 1.0, 6.0, ((0, 8), (1, 16)))
    projection_matrix = normal_values(key_of[2], (POOLED_WIDTH, EMBED_WIDTH), POOLED_WIDTH ** -0.5, 0.1875)
    lowrank_down_weight = normal_values(key_of[3], (POOLED_WIDTH, ADAPTER_RANK), POOLED_WIDTH ** -0.5, 0.1875)
    lowrank_up_weight = normal_values(key_of[4], (ADAPTER_RANK, EMBED_WIDTH), ADAPTER_RANK ** -0.5, 0.75)
    similarity_scale = jnp.clip(jax.random.uniform(key_of[5], (1,), jnp.float32, 2.0, 5.0), 2.0, 5.0)
    similarity_bias = jnp.clip(jax.random.uniform(key_of[6], (1,), jnp.float32, -6.0, -2.0), -6.0, -2.0)
    return dict(pooled_image_rows=pooled_image_rows, text_embed_rows=text_embed_rows, projection_matrix=projection_matrix, lowrank_down_weight=lowrank_down_weight, lowrank_up_weight=lowrank_up_weight, similarity_scale=similarity_scale, similarity_bias=similarity_bias)


def reference(pooled_image_rows, text_embed_rows, projection_matrix, lowrank_down_weight, lowrank_up_weight, similarity_scale, similarity_bias):
    factor = similarity_scale[0] / math.sqrt(EMBED_WIDTH)
    bias = similarity_bias[0]
    eye = jnp.eye(PAIRS, dtype=bool)

    def replica(pair):
        feature_rows, texts = pair
        hidden_rows = jnp.dot(feature_rows, lowrank_down_weight, preferred_element_type=jnp.float32).astype(jnp.bfloat16)
        embed_vectors = (jnp.dot(feature_rows, projection_matrix, preferred_element_type=jnp.float32) + jnp.dot(hidden_rows, lowrank_up_weight, preferred_element_type=jnp.float32)).astype(jnp.bfloat16)
        sims = jnp.dot(embed_vectors, texts.T, preferred_element_type=jnp.float32)
        logits = factor * sims + bias
        coef = jnp.where(eye, -jax.nn.sigmoid(-logits), jax.nn.sigmoid(logits))
        weights = (coef * factor).astype(jnp.bfloat16)
        text_grad = jnp.dot(weights.T, embed_vectors, preferred_element_type=jnp.float32)
        image_gradient = jnp.dot(weights, texts, preferred_element_type=jnp.float32).astype(jnp.bfloat16)
        inner_product = jnp.dot(image_gradient, lowrank_up_weight.T, preferred_element_type=jnp.float32).astype(jnp.bfloat16)
        part_up = jnp.dot(hidden_rows.T, image_gradient, preferred_element_type=jnp.float32)
        part_down = jnp.dot(feature_rows.T, inner_product, preferred_element_type=jnp.float32)
        return (text_grad, part_down, part_up)
    text_grad, parts_down, parts_up = lax.map(replica, (pooled_image_rows, text_embed_rows))
    grad_down = lax.optimization_barrier(jnp.sum(parts_down, axis=0)) / PAIRS
    grad_up = lax.optimization_barrier(jnp.sum(parts_up, axis=0)) / PAIRS
    return (text_grad, grad_down, grad_up)
```

```python
import math

import jax
import jax.numpy as jnp
from jax import lax
from jax.sharding import Mesh, PartitionSpec as P

F32, BF16, F16 = jnp.float32, jnp.bfloat16, jnp.float16
AXES = ("z", "y", "c", "h", "x")
HEIGHT = 1024.0


def from_ahead(block, axis, distance):
    n = lax.axis_size(axis)
    return lax.ppermute(block, axis, [((i + distance) % n, i) for i in range(n)])


def mm(a, b):
    return jnp.dot(a, b, preferred_element_type=F32)


def mm_nt(a, b):
    return lax.dot_general(a, b, (((1,), (1,)), ((), ())), preferred_element_type=F32)


def mm_tn(a, b):
    return lax.dot_general(a, b, (((0,), (0,)), ((), ())), preferred_element_type=F32)


def halves(a):
    high = a.astype(BF16)
    return high, (a - high.astype(F32)).astype(BF16)


def scatter_sum(block, axis):
    n, here, part = 4, lax.axis_index(axis), block.shape[0] // 4
    piece = lambda d: lax.dynamic_slice_in_dim(block, ((here - d) % n) * part, part, 0)
    others = [from_ahead(piece(d), axis, d) for d in (1, 3, 2)]
    return piece(0) + others[0] + others[1] + others[2]


def gathered(block, axis):
    n, here, part = 4, lax.axis_index(axis), block.shape[0]
    whole = jnp.zeros((n * part,) + block.shape[1:], block.dtype)
    others = [(0, block)] + [(d, from_ahead(block, axis, d)) for d in (1, 3, 2)]
    for d, other in others:
        whole = lax.dynamic_update_slice_in_dim(whole, other, ((here + d) % n) * part, 0)
    return whole


def everyones(block, axis):
    return block + from_ahead(block, axis, 1) + from_ahead(block, axis, 3) + from_ahead(block, axis, 2)


def shards(images, texts, proj, down, up, scale, offset):
    own, texts = images[0], texts[0]
    rows, width = texts.shape
    half = rows // 2
    factor = scale[0] / math.sqrt(width)
    bias = offset[0]
    core = lax.axis_index("c")

    ahead = from_ahead(own, "z", 1)
    behind = from_ahead(own, "z", -1)
    across = from_ahead(texts, "y", 1)
    twin = from_ahead(texts, "c", 1)
    across_twin = from_ahead(across, "c", 1)
    far = jnp.concatenate([from_ahead(ahead[:half], "z", 1), from_ahead(behind[half:], "z", -1)])

    near_pair = jnp.concatenate([texts, twin])
    far_pair = jnp.concatenate([across, across_twin])
    group = jnp.concatenate([near_pair, far_pair])
    text_up = jnp.concatenate(halves(mm_nt(group, up)), axis=1)

    def embedded(block):
        hidden = mm(block, down).astype(BF16)
        return hidden, (mm(block, proj) + mm(hidden, up)).astype(BF16)

    def weights_of(columns, embeds, same=False):
        logits = factor * mm_nt(columns, embeds) + bias
        coef = jax.nn.sigmoid(logits)
        if same:
            row = lax.broadcasted_iota(jnp.int32, logits.shape, 0)
            col = lax.broadcasted_iota(jnp.int32, logits.shape, 1)
            coef = jnp.where(row == col, -jax.nn.sigmoid(-logits), coef)
        return (coef * factor).astype(BF16)

    def share(block, hidden, weights):
        inner = mm_tn(weights, text_up)
        rank = inner.shape[1] // 2
        inner = jnp.concatenate(halves(inner[:, :rank] + inner[:, rank:]), axis=1)
        grad = mm_tn(inner, block)
        return grad[:rank] + grad[rank:], mm(weights, hidden)

    hidden, embeds = embedded(own)
    near = weights_of(near_pair, embeds, True)
    weights = jnp.concatenate([near, weights_of(far_pair, embeds)])
    part_down, hidden_sum = share(own, hidden, weights)
    text_sum = mm(weights, embeds)

    sides = jnp.concatenate([ahead, behind])
    hidden, embeds = embedded(sides)
    weights = weights_of(group, embeds)
    d, h = share(sides, hidden, weights)
    part_down, hidden_sum = part_down + d, hidden_sum + h
    text_sum = text_sum + mm(weights, embeds)

    hidden, embeds = embedded(far)
    weights = weights_of(group, embeds)
    d, h = share(far, hidden, weights)
    part_down, hidden_sum = part_down + d, hidden_sum + h
    rank = hidden_sum.shape[1]
    part_up = mm_tn(jnp.concatenate(halves(hidden_sum), axis=1), group)
    part_up = part_up[:rank] + part_up[rank:]

    first = core == 0
    kept = jnp.where(first, part_down, part_up)
    kept = kept + from_ahead(jnp.where(first, part_up, part_down), "c", 1)
    kept = scatter_sum(kept, "z")
    kept = everyones(kept, "x")
    kept = everyones(kept, ("y", "h"))
    kept = gathered(kept, "z") / (rows * 16)
    other = from_ahead(kept, "c", 1)
    grad_down = jnp.where(first, kept, other).T
    grad_up = jnp.where(first, other, kept)

    text_sum = text_sum + mm(weights, embeds)
    away = text_sum[2 * rows : 3 * rows] + from_ahead(text_sum[3 * rows :], "c", 1)
    height = jnp.maximum(jnp.max(jnp.abs(away), axis=1, keepdims=True), 1e-30)
    packed = (away * (HEIGHT / height)).astype(F16)
    packed = from_ahead(packed, "y", 1)
    height = from_ahead(jnp.broadcast_to(height, (rows, 128)), "y", 1)[:, :1]
    text_grad = text_sum[:rows] + from_ahead(text_sum[rows : 2 * rows], "c", 1)
    text_grad = text_grad + packed.astype(F32) * (height / HEIGHT)
    return text_grad[None], grad_down, grad_up


def solution(mesh):
    grid = Mesh(mesh.devices.reshape(4, 2, 2, 2, 4), AXES)
    blk, dp = ("z", "y", "c"), ("h", "x")
    placed = (P(dp, blk, None), P(dp, blk, None), P(), P(), P(), P(), P())
    return jax.shard_map(
        shards,
        mesh=grid,
        in_specs=placed,
        out_specs=(P(dp, blk, None), P(), P()),
        check_vma=False,
    )
```

```python
import math

import jax
import jax.numpy as jnp
from jax import lax
from jax.experimental import pallas as pl
from jax.experimental.pallas import tpu as pltpu
from jax.sharding import Mesh, PartitionSpec as P

F32, BF16, F16 = jnp.float32, jnp.bfloat16, jnp.float16
AXES = ("z", "y", "c", "h", "x")
LOG2E = 1.4426950408889634
HEIGHT = 1024.0
MIB = 1 << 20


def from_ahead(block, axis, distance):
    n = lax.axis_size(axis)
    return lax.ppermute(block, axis, [((i + distance) % n, i) for i in range(n)])


def mm(a, b):
    return jnp.dot(a, b, preferred_element_type=F32)


def mm_nt(a, b):
    return lax.dot_general(a, b, (((1,), (1,)), ((), ())), preferred_element_type=F32)


def mm_tn(a, b):
    return lax.dot_general(a, b, (((0,), (0,)), ((), ())), preferred_element_type=F32)


def halves(a):
    high = a.astype(BF16)
    return high, (a - high.astype(F32)).astype(BF16)


def embed(images, at, both, proj, down, up):
    here = slice(at, at + images.shape[0])
    width, rank = proj.shape[1], down.shape[1]
    hidden = mm(images[...], down[...]).astype(BF16)
    both[here, :width] = (mm(images[...], proj[...]) + mm(hidden, up[...])).astype(BF16)
    both[here, width : width + rank] = hidden
    both[here, width + rank :] = jnp.zeros((images.shape[0], both.shape[1] - width - rank), BF16)


def gate(sims, consts):
    power = jnp.minimum(sims * consts[0] + consts[1], 126.0)
    return (consts[2] / (1.0 + jnp.exp2(power))).astype(BF16)


def gate_matching(sims, consts):
    power = sims * consts[0] + consts[1]
    other = consts[2] / (1.0 + jnp.exp2(jnp.minimum(power, 126.0)))
    match = -consts[2] / (1.0 + jnp.exp2(jnp.minimum(-power, 126.0)))
    row = lax.broadcasted_iota(jnp.int32, sims.shape, 0)
    col = lax.broadcasted_iota(jnp.int32, sims.shape, 1)
    return jnp.where(row == col, match, other).astype(BF16)


def text_ups(texts, up, out, at):
    high, low = halves(mm_nt(up[...], texts[...]))
    out[:, at : at + texts.shape[0]] = jnp.concatenate([high, low])


def down_share(inner, images):
    rank = inner.shape[0] // 2
    pair = jnp.concatenate(halves(inner[:rank] + inner[rank:]))
    grad = mm(pair, images)
    return grad[:rank] + grad[rank:]


def own_kernel(consts, own, t0, t1, proj, down, up, both, ups, s0, s1, h0, h1, inner, w):
    width, rows = proj.shape[1], own.shape[0]
    embed(own, 0, both, proj, down, up)
    for k, (texts, s, h) in enumerate(((t0, s0, h0), (t1, s1, h1))):
        text_ups(texts, up, ups, k * rows)
        sims = mm_nt(texts[...], both[:, :width])
        w[...] = gate(sims, consts) if k else gate_matching(sims, consts)
        sums = mm(w[...], both[...])
        s[...], h[...] = sums[:, :width], sums[:, width:]
        part = mm(ups[:, k * rows : (k + 1) * rows], w[...])
        inner[...] = inner[...] + part if k else part


def side_kernel(consts, a, b, t0, t1, ups, proj, down, up, s0, s1, h0, h1, both, o0, o1, g0, g1, inner, w):
    width, rows = proj.shape[1], a.shape[0]
    embed(a, 0, both, proj, down, up)
    embed(b, rows, both, proj, down, up)
    for k, (texts, s, h, o, g) in enumerate(((t0, s0, h0, o0, g0), (t1, s1, h1, o1, g1))):
        w[...] = gate(mm_nt(texts[...], both[:, :width]), consts)
        sums = mm(w[...], both[...])
        o[...], g[...] = s[...] + sums[:, :width], h[...] + sums[:, width:]
        part = mm(ups[:, k * rows : (k + 1) * rows], w[...])
        inner[...] = inner[...] + part if k else part


def far_text_kernel(consts, both0, both1, t0, t1, up, inner0, inner1, own, a, b, ups, s0, s1, h0, h1, grad, w0, w1):
    rows, width = own.shape
    sums0, sums1 = inner0[...], inner1[...]
    for k, (texts, s, h) in enumerate(((t0, s0, h0), (t1, s1, h1))):
        text_ups(texts, up, ups, k * rows)
        w0[...] = gate(mm_nt(texts[...], both0[:, :width]), consts)
        w1[...] = gate(mm_nt(texts[...], both1[:, :width]), consts)
        sums = mm(w0[...], both0[...]) + mm(w1[...], both1[...])
        s[...], h[...] = sums[:, :width], sums[:, width:]
        mine = ups[:, k * rows : (k + 1) * rows]
        sums0, sums1 = sums0 + mm(mine, w0[...]), sums1 + mm(mine, w1[...])
    grad[...] = down_share(sums0, own[...]) + down_share(sums1[:, :rows], a[...]) + down_share(sums1[:, rows:], b[...])


def last_kernel(consts, fa, fb, t0, t1, t2, t3, ups0, ups1, proj, down, up, h0, h1, h2, h3, grad, parts, both, w):
    half, rows, width, rank = fa.shape[0], t0.shape[0], proj.shape[1], down.shape[1]
    embed(fa, 0, both, proj, down, up)
    embed(fb, half, both, proj, down, up)
    inner, grad_up = None, None
    for k, (texts, h) in enumerate(((t0, h0), (t1, h1), (t2, h2), (t3, h3))):
        here = slice(k * rows, (k + 1) * rows)
        w[here] = gate(mm_nt(texts[...], both[:, :width]), consts)
        hidden = h[...] + mm(w[here], both[:, width:])
        high, low = halves(hidden[:, :rank])
        share = mm_tn(jnp.concatenate([high, low], axis=1), texts[...])
        ups = ups0 if k < 2 else ups1
        part = mm(ups[:, (k % 2) * rows : (k % 2 + 1) * rows], w[here])
        inner = part if inner is None else inner + part
        grad_up = share if grad_up is None else grad_up + share
    parts[:rank] = grad[...] + down_share(inner[:, :half], fa[...]) + down_share(inner[:, half:], fb[...])
    parts[rank:] = grad_up[:rank] + grad_up[rank:]


def add_kernel(first, w, both, s0, s1, o0, o1):
    rows, width = s0.shape
    for k, (s, o) in enumerate(((s0, o0), (s1, o1))):
        at = (first + k) * rows
        o[...] = s[...] + mm(w[at : at + rows], both[:, :width])


def run(kernel, name, operands, outs, scratch, flops, consts=True):
    spec = pl.BlockSpec(memory_space=pltpu.VMEM)
    ins = [spec] * len(operands)
    if consts:
        ins[0] = pl.BlockSpec(memory_space=pltpu.SMEM)
    size = sum(math.prod(o.shape) * o.dtype.itemsize for o in list(operands) + list(outs))
    return pl.pallas_call(
        kernel,
        in_specs=ins,
        out_specs=[spec] * len(outs),
        out_shape=outs,
        scratch_shapes=scratch,
        compiler_params=pltpu.CompilerParams(vmem_limit_bytes=30 * MIB),
        cost_estimate=pl.CostEstimate(flops=int(flops), bytes_accessed=size, transcendentals=0),
        name=name,
    )(*operands)


def scatter_sum(block, axis):
    n, here, part = 4, lax.axis_index(axis), block.shape[0] // 4
    piece = lambda d: lax.dynamic_slice_in_dim(block, ((here - d) % n) * part, part, 0)
    others = [from_ahead(piece(d), axis, d) for d in (1, 3, 2)]
    return piece(0) + others[0] + others[1] + others[2]


def gathered(block, axis):
    n, here, part = 4, lax.axis_index(axis), block.shape[0]
    whole = jnp.zeros((n * part,) + block.shape[1:], block.dtype)
    others = [(0, block)] + [(d, from_ahead(block, axis, d)) for d in (1, 3, 2)]
    for d, other in others:
        whole = lax.dynamic_update_slice_in_dim(whole, other, ((here + d) % n) * part, 0)
    return whole


def everyones(block, axis):
    return block + from_ahead(block, axis, 1) + from_ahead(block, axis, 3) + from_ahead(block, axis, 2)


def shards(images, texts, proj, down, up, scale, offset):
    own, texts = images[0], texts[0]
    rows, width = texts.shape
    rank = down.shape[1]
    half, wide = rows // 2, width + 128
    factor = scale[0] / math.sqrt(width)
    consts = jnp.stack([-factor * LOG2E, -offset[0] * LOG2E, factor])
    core = lax.axis_index("c")

    twin = from_ahead(texts, "c", 1)
    ahead = from_ahead(own, "z", 1)
    behind = from_ahead(own, "z", -1)
    across = from_ahead(texts, "y", 1)
    far_a = from_ahead(ahead[:half], "z", 1)
    far_b = from_ahead(behind[half:], "z", -1)
    across_twin = from_ahead(across, "c", 1)

    shape = jax.ShapeDtypeStruct
    sums, narrow = shape((rows, width), F32), shape((rows, 128), F32)
    unit = 2.0 * rows * rows * width
    pair_flops = 2.2 * unit

    both0, ups0, s0, s1, h0, h1, inner0 = run(
        own_kernel,
        "own_rows",
        [consts, own, texts, twin, proj, down, up],
        [shape((rows, wide), BF16), shape((2 * rank, 2 * rows), BF16), sums, sums, narrow, narrow, shape((2 * rank, rows), F32)],
        [pltpu.VMEM((rows, rows), BF16)],
        3.2 * unit + 2 * pair_flops,
    )
    both1, s0, s1, h0, h1, inner1 = run(
        side_kernel,
        "side_rows",
        [consts, ahead, behind, texts, twin, ups0, proj, down, up, s0, s1, h0, h1],
        [shape((2 * rows, wide), BF16), sums, sums, narrow, narrow, shape((2 * rank, 2 * rows), F32)],
        [pltpu.VMEM((rows, 2 * rows), BF16)],
        6.4 * unit + 4 * pair_flops,
    )
    ups1, s2, s3, h2, h3, grad = run(
        far_text_kernel,
        "far_texts",
        [consts, both0, both1, across, across_twin, up, inner0, inner1, own, ahead, behind],
        [shape((2 * rank, 2 * rows), BF16), sums, sums, narrow, narrow, shape((rank, width), F32)],
        [pltpu.VMEM((rows, rows), BF16), pltpu.VMEM((rows, 2 * rows), BF16)],
        6 * pair_flops,
    )
    parts, both2, weights = run(
        last_kernel,
        "far_rows",
        [consts, far_a, far_b, texts, twin, across, across_twin, ups0, ups1, proj, down, up, h0, h1, h2, h3, grad],
        [shape((2 * rank, width), F32), shape((rows, wide), BF16), shape((4 * rows, rows), BF16)],
        [],
        3.2 * unit + 5 * unit,
    )

    kept = lax.dynamic_slice_in_dim(parts, core * rank, rank, 0)
    kept = kept + from_ahead(lax.dynamic_slice_in_dim(parts, (1 - core) * rank, rank, 0), "c", 1)
    kept = scatter_sum(kept, "z")
    kept = everyones(kept, "x")
    kept = everyones(kept, ("y", "h"))
    kept = gathered(kept, "z") / (rows * 16)
    other = from_ahead(kept, "c", 1)
    first = core == 0
    grad_down = jnp.where(first, kept, other).T
    grad_up = jnp.where(first, other, kept)

    s2, s3 = run(
        lambda *refs: add_kernel(2, *refs), "far_sums", [weights, both2, s2, s3], [sums, sums], [], 2 * unit, False
    )
    s0, s1 = run(
        lambda *refs: add_kernel(0, *refs), "near_sums", [weights, both2, s0, s1], [sums, sums], [], 2 * unit, False
    )
    away = s2 + from_ahead(s3, "c", 1)
    height = jnp.maximum(jnp.max(jnp.abs(away), axis=1, keepdims=True), 1e-30)
    packed = (away * (HEIGHT / height)).astype(F16)
    packed = from_ahead(packed, "y", 1)
    height = from_ahead(jnp.broadcast_to(height, (rows, 128)), "y", 1)[:, :1]
    text_grad = s0 + from_ahead(s1, "c", 1) + packed.astype(F32) * (height / HEIGHT)
    return text_grad[None], grad_down, grad_up


def solution(mesh):
    grid = Mesh(mesh.devices.reshape(4, 2, 2, 2, 4), AXES)
    blk, dp = ("z", "y", "c"), ("h", "x")
    placed = (P(dp, blk, None), P(dp, blk, None), P(), P(), P(), P(), P())
    return jax.shard_map(
        shards,
        mesh=grid,
        in_specs=placed,
        out_specs=(P(dp, blk, None), P(), P()),
        check_vma=False,
    )
```

```python
import functools
import math

import jax
import jax.numpy as jnp
from jax import lax
from jax.experimental import pallas as pl
from jax.experimental.pallas import tpu as pltpu
from jax.sharding import Mesh, PartitionSpec as P

F32, BF16, F16 = jnp.float32, jnp.bfloat16, jnp.float16
AXES = ("z", "y", "c", "h", "x")
LOG2E = 1.4426950408889634
REACH = 14.0
MIB = 1 << 20


def tied(*values):
    return lax.optimization_barrier(values)


def from_ahead(block, axis, distance):
    n = lax.axis_size(axis)
    return lax.ppermute(block, axis, [((i + distance) % n, i) for i in range(n)])


def mm(a, b):
    return jnp.dot(a, b, preferred_element_type=F32)


def mm_nt(a, b):
    return lax.dot_general(a, b, (((1,), (1,)), ((), ())), preferred_element_type=F32)


def mm_tn(a, b):
    return lax.dot_general(a, b, (((0,), (0,)), ((), ())), preferred_element_type=F32)


def halves(a):
    high = a.astype(BF16)
    return high, (a - high.astype(F32)).astype(BF16)


def embed(images, at, both, proj, down, up):
    here = slice(at, at + images.shape[0])
    width, rank = proj.shape[1], down.shape[0]
    hidden = mm_nt(images[...], down[...]).astype(BF16)
    both[here, :width] = (mm(images[...], proj[...]) + mm(hidden, up[...])).astype(BF16)
    both[here, width : width + rank] = hidden
    both[here, width + rank :] = jnp.zeros((images.shape[0], both.shape[1] - width - rank), BF16)


def gate(sims, consts):
    power = jnp.minimum(sims * consts[0] + consts[1], 126.0)
    return (consts[2] / (1.0 + jnp.exp2(power))).astype(BF16)


def gate_matching(sims, consts):
    power = sims * consts[0] + consts[1]
    other = consts[2] / (1.0 + jnp.exp2(jnp.minimum(power, 126.0)))
    match = -consts[2] / (1.0 + jnp.exp2(jnp.minimum(-power, 126.0)))
    row = lax.broadcasted_iota(jnp.int32, sims.shape, 0)
    col = lax.broadcasted_iota(jnp.int32, sims.shape, 1)
    return jnp.where(row == col, match, other).astype(BF16)


def text_ups(texts, up, out, at):
    high, low = halves(mm_nt(up[...], texts[...]))
    out[:, at : at + texts.shape[0]] = jnp.concatenate([high, low])


def down_share(inner, images):
    rank = inner.shape[0] // 2
    pair = jnp.concatenate(halves(inner[:rank] + inner[rank:]))
    grad = mm(pair, images)
    return grad[:rank] + grad[rank:]


def up_share(hidden, texts, rank):
    pair = jnp.concatenate(halves(hidden[:, :rank]), axis=1)
    grad = mm_tn(pair, texts)
    return grad[:rank] + grad[rank:]


def own_kernel(consts, own, t0, t1, proj, down, up, both, ups, s0, s1, h0, h1, inner, w):
    width, rows = proj.shape[1], own.shape[0]
    embed(own, 0, both, proj, down, up)
    for k, (texts, s, h) in enumerate(((t0, s0, h0), (t1, s1, h1))):
        text_ups(texts, up, ups, k * rows)
        sims = mm_nt(texts[...], both[:, :width])
        w[...] = gate(sims, consts) if k else gate_matching(sims, consts)
        sums = mm(w[...], both[...])
        s[...], h[...] = sums[:, :width], sums[:, width:]
        part = mm(ups[:, k * rows : (k + 1) * rows], w[...])
        inner[...] = inner[...] + part if k else part


def side_kernel(consts, a, b, t0, t1, ups, proj, down, up, s0, s1, h0, h1, both, o0, o1, g0, g1, inner, w):
    width, rows = proj.shape[1], a.shape[0]
    embed(a, 0, both, proj, down, up)
    embed(b, rows, both, proj, down, up)
    for k, (texts, s, h, o, g) in enumerate(((t0, s0, h0, o0, g0), (t1, s1, h1, o1, g1))):
        w[...] = gate(mm_nt(texts[...], both[:, :width]), consts)
        sums = mm(w[...], both[...])
        o[...], g[...] = s[...] + sums[:, :width], h[...] + sums[:, width:]
        part = mm(ups[:, k * rows : (k + 1) * rows], w[...])
        inner[...] = inner[...] + part if k else part


def far_text_kernel(
    consts, both0, both1, t0, t1, up, inner0, inner1, own, a, b, near, h1, ups, s0, s1, h0, grad_down, grad_up, w0, w1
):
    rows, width = own.shape
    rank = up.shape[0]
    sums0, sums1 = inner0[...], inner1[...]
    for k, (texts, s) in enumerate(((t0, s0), (t1, s1))):
        text_ups(texts, up, ups, k * rows)
        w0[...] = gate(mm_nt(texts[...], both0[:, :width]), consts)
        w1[...] = gate(mm_nt(texts[...], both1[:, :width]), consts)
        sums = mm(w0[...], both0[...]) + mm(w1[...], both1[...])
        s[...] = sums[:, :width]
        if k == 0:
            h0[...] = sums[:, width:]
        else:
            grad_up[...] = up_share(sums[:, width:], texts[...], rank) + up_share(h1[...], near[...], rank)
        mine = ups[:, k * rows : (k + 1) * rows]
        sums0, sums1 = sums0 + mm(mine, w0[...]), sums1 + mm(mine, w1[...])
    grad_down[...] = (
        down_share(sums0, own[...]) + down_share(sums1[:, :rows], a[...]) + down_share(sums1[:, rows:], b[...])
    )


def last_kernel(
    consts, far, far_twin, t0, t1, ups0, ups1, proj, down, up, h0, h1, grad_down, grad_up, kept, sent, both, w0, w1
):
    rows, width, rank = t0.shape[0], proj.shape[1], up.shape[0]
    at, blocks = 0, (far, far_twin)
    for block in blocks:
        embed(block, at, both, proj, down, up)
        at += block.shape[0]
    inner, up_sum = None, grad_up[...]
    for texts, ups, h, w in ((t0, ups0, h0, w0), (t1, ups1, h1, w1)):
        w[...] = gate(mm_nt(texts[...], both[:, :width]), consts)
        up_sum = up_sum + up_share(h[...] + mm(w[...], both[:, width:]), texts[...], rank)
        part = mm(ups[:, :rows], w[...])
        inner = part if inner is None else inner + part
    down_sum, at = grad_down[...], 0
    for block in blocks:
        down_sum = down_sum + down_share(inner[:, at : at + block.shape[0]], block[...])
        at += block.shape[0]
    first = lax.axis_index("c") == 0
    kept[...] = jnp.where(first, down_sum, up_sum)
    sent[...] = jnp.where(first, up_sum, down_sum)


def near_kernel(w, both, s, twin, out):
    out[...] = s[...] + twin[...] + mm(w[...], both[:, : s.shape[1]])


def away_kernel(w, both, s, twin, *outs):
    rows, width = s.shape
    value = s[...] + twin[...] + mm(w[...], both[:, :width])
    top = jnp.maximum(jnp.max(jnp.abs(value), keepdims=True), 1e-30)
    power = jnp.ceil(jnp.log2(top))
    value = value * jnp.exp2(REACH - power)
    part = rows // len(outs)
    for k, out in enumerate(outs):
        out[:part] = value[k * part : (k + 1) * part]
        if k == 0:
            out[part:] = jnp.broadcast_to(power, (out.shape[0] - part, width))


def finish_kernel(near, c0, c1, c2, c3, out):
    part = c1.shape[0]
    scale = jnp.exp2(c0[part : part + 1, :] - REACH)
    for k, chunk in enumerate((c0, c1, c2, c3)):
        here = slice(k * part, (k + 1) * part)
        out[here] = near[here] + chunk[:part] * scale


def quarter_kernel(a, b, o0, o1, o2, o3, total):
    total[...] = a[...] + b[...]
    here, part = lax.axis_index("z"), o0.shape[0]
    for out, d in ((o0, 0), (o1, 1), (o2, 3), (o3, 2)):
        out[...] = total[pl.ds(pl.multiple_of(((here + 4 - d) % 4) * part, part), part), :]


def sum_kernel(a, b, c, d, out):
    out[...] = a[...] + b[...] + c[...] + d[...]


def place_kernel(pairs, a, b, c, d, out):
    here, part = lax.axis_index("z"), a.shape[0]
    for block, k in ((a, 0), (b, 1), (c, 3), (d, 2)):
        out[pl.ds(pl.multiple_of(((here + k) % 4) * part, part), part), :] = block[...] / pairs


def join_kernel(a, b, down, up):
    first = lax.axis_index("c") == 0
    down[...] = jnp.where(first, a[...], b[...])
    up[...] = jnp.where(first, b[...], a[...])


def run(kernel, name, operands, outs, scratch, flops, consts=True):
    spec = pl.BlockSpec(memory_space=pltpu.VMEM)
    ins = [spec] * len(operands)
    if consts:
        ins[0] = pl.BlockSpec(memory_space=pltpu.SMEM)
    size = sum(math.prod(o.shape) * o.dtype.itemsize for o in list(operands) + list(outs))
    return pl.pallas_call(
        kernel,
        in_specs=ins,
        out_specs=[spec] * len(outs),
        out_shape=outs,
        scratch_shapes=scratch,
        compiler_params=pltpu.CompilerParams(vmem_limit_bytes=16 * MIB),
        cost_estimate=pl.CostEstimate(flops=int(flops), bytes_accessed=size, transcendentals=0),
        name=name,
    )(*operands)


def shards(images, texts, proj, down, up, scale, offset):
    own, texts = images[0], texts[0]
    rows, width = texts.shape
    rank = down.shape[1]
    wide = width + 128
    factor = scale[0] / math.sqrt(width)
    consts = jnp.stack([-factor * LOG2E, -offset[0] * LOG2E, factor])
    down = down.T

    def turned(block, way):
        n = lax.axis_size("z")
        step = lambda z, c: (z + (way if c == 0 else -way)) % n
        return lax.ppermute(block, ("z", "c"), [(2 * step(z, c) + c, 2 * z + c) for z in range(n) for c in range(2)])

    twin = from_ahead(texts, "c", 1)
    ahead = turned(own, 1)
    behind = turned(own, -1)
    across = from_ahead(texts, "y", 1)

    shape = jax.ShapeDtypeStruct
    sums, narrow, grads = shape((rows, width), F32), shape((rows, 128), F32), shape((rank, width), F32)
    unit = 2.0 * rows * rows * width
    pair_flops = 2.2 * unit

    both0, ups0, s0, s1, h0, h1, inner0 = run(
        own_kernel,
        "own_rows",
        [consts, own, texts, twin, proj, down, up],
        [shape((rows, wide), BF16), shape((2 * rank, 2 * rows), BF16), sums, sums, narrow, narrow, shape((2 * rank, rows), F32)],
        [pltpu.VMEM((rows, rows), BF16)],
        3.2 * unit + 2 * pair_flops,
    )
    ups0, across, ahead, behind = tied(ups0, across, ahead, behind)
    far = turned(ahead, 1)
    across_twin = from_ahead(across, "c", 1)
    both1, s0, s1, h0, h1, inner1 = run(
        side_kernel,
        "side_rows",
        [consts, ahead, behind, texts, twin, ups0, proj, down, up, s0, s1, h0, h1],
        [shape((2 * rows, wide), BF16), sums, sums, narrow, narrow, shape((2 * rank, 2 * rows), F32)],
        [pltpu.VMEM((rows, 2 * rows), BF16)],
        6.4 * unit + 4 * pair_flops,
    )
    ups1, s2, s3, h2, grad_down, grad_up = run(
        far_text_kernel,
        "far_texts",
        [consts, both0, both1, across, across_twin, up, inner0, inner1, own, ahead, behind, twin, h1],
        [shape((2 * rank, 2 * rows), BF16), sums, sums, narrow, grads, grads],
        [pltpu.VMEM((rows, rows), BF16), pltpu.VMEM((rows, 2 * rows), BF16)],
        6 * pair_flops,
    )
    far_twin = from_ahead(far, "c", 1)
    s1 = from_ahead(s1, "c", 1)
    s3 = from_ahead(s3, "c", 1)
    kept, sent, both2, w0, w2 = run(
        last_kernel,
        "far_rows",
        [consts, far, far_twin, texts, across, ups0, ups1, proj, down, up, h0, h2, grad_down, grad_up],
        [grads, grads, shape((2 * rows, wide), BF16)] + [shape((rows, 2 * rows), BF16)] * 2,
        [],
        6.4 * unit + 5 * unit,
    )

    def small(kernel, name, operands, outs, scratch=()):
        return run(kernel, name, operands, outs, scratch, 1, False)

    part = rows // 4
    chunks = small(
        away_kernel, "away_sums", [w2, both2, s2, s3], [shape((part + (16 if k == 0 else 0), width), F32) for k in range(4)]
    )
    chunks = [chunk.astype(F16) for chunk in chunks]

    def beside(k, value):
        moved = from_ahead(chunks[k], "y", 1).astype(F32)
        return tied(value, moved)

    def everyones(block, axis):
        others = [from_ahead(block, axis, d) for d in (1, 3, 2)]
        return small(sum_kernel, "sums", [block] + others, [quarter])[0]

    quarter = shape((rank // 4, width), F32)
    sent = from_ahead(sent, "c", 1)
    sent, *chunks = tied(sent, *chunks)
    pieces = small(quarter_kernel, "quarters", [kept, sent], [quarter] * 4, [pltpu.VMEM((rank, width), F32)])
    pieces = [pieces[0]] + [from_ahead(p, "z", d) for p, d in zip(pieces[1:], (1, 3, 2))]
    (kept,) = small(sum_kernel, "sums", pieces, [quarter])
    kept, c0 = beside(0, kept)
    kept = everyones(kept, "x")
    kept, c1 = beside(1, kept)
    (near,) = small(near_kernel, "near_sums", [w0, both2, s0, s1], [sums])
    kept, near = tied(kept, near)
    kept = everyones(kept, ("y", "h"))
    kept, c2 = beside(2, kept)
    pieces = [kept] + [from_ahead(kept, "z", d) for d in (1, 3, 2)]
    (kept,) = small(functools.partial(place_kernel, float(rows * 16)), "places", pieces, [grads])
    kept, c3 = beside(3, kept)
    other = from_ahead(kept, "c", 1)
    (text_grad,) = small(finish_kernel, "finish", [near, c0, c1, c2, c3], [sums])
    grad_down, grad_up = small(join_kernel, "joined", [kept, other], [grads, grads])
    grad_down = grad_down.T
    return text_grad[None], grad_down, grad_up


def solution(mesh):
    grid = Mesh(mesh.devices.reshape(4, 2, 2, 2, 4), AXES)
    blk, dp = ("z", "y", "c"), ("h", "x")
    placed = (P(dp, blk, None), P(dp, blk, None), P(), P(), P(), P(), P())
    return jax.shard_map(
        shards,
        mesh=grid,
        in_specs=placed,
        out_specs=(P(dp, blk, None), P(), P()),
        check_vma=False,
    )
```

```python
import functools
import math

import jax
import jax.numpy as jnp
from jax import lax
from jax.experimental import pallas as pl
from jax.experimental.pallas import tpu as pltpu
from jax.sharding import Mesh, PartitionSpec as P

F32, BF16, F16 = jnp.float32, jnp.bfloat16, jnp.float16
AXES = ("z", "y", "c", "h", "x")
LOG2E = 1.4426950408889634
REACH = 14.0
MIB = 1 << 20


def tied(*values):
    return lax.optimization_barrier(values)


def from_ahead(block, axis, distance):
    n = lax.axis_size(axis)
    return lax.ppermute(block, axis, [((i + distance) % n, i) for i in range(n)])


def mm(a, b):
    return jnp.dot(a, b, preferred_element_type=F32)


def mm_nt(a, b):
    return lax.dot_general(a, b, (((1,), (1,)), ((), ())), preferred_element_type=F32)


def mm_tn(a, b):
    return lax.dot_general(a, b, (((0,), (0,)), ((), ())), preferred_element_type=F32)


def halves(a):
    high = a.astype(BF16)
    return high, (a - high.astype(F32)).astype(BF16)


def embed(images, at, both, proj, down, up):
    here = slice(at, at + images.shape[0])
    width, rank = proj.shape[1], down.shape[0]
    hidden = mm_nt(images[...], down[...]).astype(BF16)
    both[here, :width] = (mm(images[...], proj[...]) + mm(hidden, up[...])).astype(BF16)
    both[here, width : width + rank] = hidden
    both[here, width + rank :] = jnp.zeros((images.shape[0], both.shape[1] - width - rank), BF16)


def gate(sims, consts):
    power = jnp.minimum(sims * consts[0] + consts[1], 126.0)
    return (consts[2] / (1.0 + jnp.exp2(power))).astype(BF16)


def gate_matching(sims, consts):
    power = sims * consts[0] + consts[1]
    other = consts[2] / (1.0 + jnp.exp2(jnp.minimum(power, 126.0)))
    match = -consts[2] / (1.0 + jnp.exp2(jnp.minimum(-power, 126.0)))
    row = lax.broadcasted_iota(jnp.int32, sims.shape, 0)
    col = lax.broadcasted_iota(jnp.int32, sims.shape, 1)
    return jnp.where(row == col, match, other).astype(BF16)


def text_ups(texts, up, out, at):
    high, low = halves(mm_nt(up[...], texts[...]))
    out[:, at : at + texts.shape[0]] = jnp.concatenate([high, low])


def down_share(inner, images):
    rank = inner.shape[0] // 2
    pair = jnp.concatenate(halves(inner[:rank] + inner[rank:]))
    grad = mm(pair, images)
    return grad[:rank] + grad[rank:]


def up_share(hidden, texts, rank):
    pair = jnp.concatenate(halves(hidden[:, :rank]), axis=1)
    grad = mm_tn(pair, texts)
    return grad[:rank] + grad[rank:]


def consts_kernel(root, scale, offset, out):
    factor = scale[0] / root
    out[0] = -factor * LOG2E
    out[1] = -offset[0] * LOG2E
    out[2] = factor


def own_kernel(consts, own, t0, t1, proj, down, up, both, ups, s0, s1, h0, h1, inner, w):
    width, rows = proj.shape[1], own.shape[0]
    embed(own, 0, both, proj, down, up)
    for k, (texts, s, h) in enumerate(((t0, s0, h0), (t1, s1, h1))):
        text_ups(texts, up, ups, k * rows)
        sims = mm_nt(texts[...], both[:, :width])
        w[...] = gate(sims, consts) if k else gate_matching(sims, consts)
        sums = mm(w[...], both[...])
        s[...], h[...] = sums[:, :width], sums[:, width:]
        part = mm(ups[:, k * rows : (k + 1) * rows], w[...])
        inner[...] = inner[...] + part if k else part


def side_kernel(consts, a, b, t0, t1, ups, proj, down, up, s0, s1, h0, h1, both, o0, o1, g0, g1, inner, w):
    width, rows = proj.shape[1], a.shape[0]
    embed(a, 0, both, proj, down, up)
    embed(b, rows, both, proj, down, up)
    for k, (texts, s, h, o, g) in enumerate(((t0, s0, h0, o0, g0), (t1, s1, h1, o1, g1))):
        w[...] = gate(mm_nt(texts[...], both[:, :width]), consts)
        sums = mm(w[...], both[...])
        o[...], g[...] = s[...] + sums[:, :width], h[...] + sums[:, width:]
        part = mm(ups[:, k * rows : (k + 1) * rows], w[...])
        inner[...] = inner[...] + part if k else part


def own_far_kernel(consts, both, texts, up, inner0, ups, s, h, inner, w):
    width = texts.shape[1]
    text_ups(texts, up, ups, 0)
    w[...] = gate(mm_nt(texts[...], both[:, :width]), consts)
    sums = mm(w[...], both[...])
    s[...], h[...] = sums[:, :width], sums[:, width:]
    inner[...] = inner0[...] + mm(ups[...], w[...])


def side_far_kernel(consts, both, texts, ups, inner0, s0, h0, s, h, inner, w):
    width = texts.shape[1]
    w[...] = gate(mm_nt(texts[...], both[:, :width]), consts)
    sums = mm(w[...], both[...])
    s[...], h[...] = s0[...] + sums[:, :width], h0[...] + sums[:, width:]
    inner[...] = inner0[...] + mm(ups[...], w[...])


def shares_kernel(inner0, inner1, own, a, b, h1, h3, t1, t3, grad_down, grad_up):
    rows, rank = own.shape[0], grad_up.shape[0]
    grad_up[...] = up_share(h1[...], t1[...], rank) + up_share(h3[...], t3[...], rank)
    grad_down[...] = (
        down_share(inner0[...], own[...])
        + down_share(inner1[:, :rows], a[...])
        + down_share(inner1[:, rows:], b[...])
    )


def last_kernel(
    consts, far, far_twin, t0, t1, ups0, ups1, proj, down, up, h0, h1, grad_down, grad_up, kept, sent, both, w0, w1
):
    rows, width, rank = t0.shape[0], proj.shape[1], up.shape[0]
    at, blocks = 0, (far, far_twin)
    for block in blocks:
        embed(block, at, both, proj, down, up)
        at += block.shape[0]
    inner, up_sum = None, grad_up[...]
    for texts, ups, h, w in ((t0, ups0, h0, w0), (t1, ups1, h1, w1)):
        w[...] = gate(mm_nt(texts[...], both[:, :width]), consts)
        up_sum = up_sum + up_share(h[...] + mm(w[...], both[:, width:]), texts[...], rank)
        part = mm(ups[:, :rows], w[...])
        inner = part if inner is None else inner + part
    down_sum, at = grad_down[...], 0
    for block in blocks:
        down_sum = down_sum + down_share(inner[:, at : at + block.shape[0]], block[...])
        at += block.shape[0]
    first = lax.axis_index("c") == 0
    kept[...] = jnp.where(first, down_sum, up_sum)
    sent[...] = jnp.where(first, up_sum, down_sum)


def near_kernel(w, both, s, twin, out):
    out[...] = s[...] + twin[...] + mm(w[...], both[:, : s.shape[1]])


def away_kernel(w, both, s, twin, *outs):
    rows, width = s.shape
    value = s[...] + twin[...] + mm(w[...], both[:, :width])
    top = jnp.maximum(jnp.max(jnp.abs(value), keepdims=True), 1e-30)
    power = jnp.ceil(jnp.log2(top))
    value = value * jnp.exp2(REACH - power)
    tail, at = outs[0].shape[0] - 16, 0
    for k, out in enumerate(outs):
        part = out.shape[0] if k else tail
        out[:part] = value[at : at + part]
        at += part
    outs[0][tail:] = jnp.broadcast_to(power, (16, width))


def finish_kernel(near, c0, c1, c2, out):
    tail, at = c0.shape[0] - 16, 0
    scale = jnp.exp2(c0[tail : tail + 1, :] - REACH)
    for k, chunk in enumerate((c0, c1, c2)):
        part = chunk.shape[0] if k else tail
        out[at : at + part] = near[at : at + part] + chunk[:part] * scale
        at += part


def quarter_kernel(a, b, o0, o1, o2, o3, total):
    total[...] = a[...] + b[...]
    here, part = lax.axis_index("z"), o0.shape[0]
    for out, d in ((o0, 0), (o1, 1), (o2, 3), (o3, 2)):
        out[...] = total[pl.ds(pl.multiple_of(((here + 4 - d) % 4) * part, part), part), :]


def sum_kernel(a, b, c, d, out):
    out[...] = a[...] + b[...] + c[...] + d[...]


def place_kernel(pairs, a, b, c, d, out):
    here, part = lax.axis_index("z"), a.shape[0]
    for block, k in ((a, 0), (b, 1), (c, 3), (d, 2)):
        out[pl.ds(pl.multiple_of(((here + k) % 4) * part, part), part), :] = block[...] / pairs


def join_kernel(a, b, down, up):
    first = lax.axis_index("c") == 0
    down[...] = jnp.where(first, a[...], b[...])
    up[...] = jnp.where(first, b[...], a[...])


def run(kernel, name, operands, outs, scratch, flops, consts=True):
    spec = pl.BlockSpec(memory_space=pltpu.VMEM)
    ins = [spec] * len(operands)
    if consts:
        ins[0] = pl.BlockSpec(memory_space=pltpu.SMEM)
    size = sum(math.prod(o.shape) * o.dtype.itemsize for o in list(operands) + list(outs))
    return pl.pallas_call(
        kernel,
        in_specs=ins,
        out_specs=[spec] * len(outs),
        out_shape=outs,
        scratch_shapes=scratch,
        compiler_params=pltpu.CompilerParams(vmem_limit_bytes=16 * MIB),
        cost_estimate=pl.CostEstimate(flops=int(flops), bytes_accessed=size, transcendentals=0),
        name=name,
    )(*operands)


def shards(images, texts, proj, down, up, scale, offset):
    own, texts = images[0], texts[0]
    rows, width = texts.shape
    rank = down.shape[1]
    wide = width + 128
    scalar = pl.BlockSpec(memory_space=pltpu.SMEM)
    consts = pl.pallas_call(
        functools.partial(consts_kernel, math.sqrt(width)),
        in_specs=[scalar, scalar],
        out_specs=scalar,
        out_shape=jax.ShapeDtypeStruct((3,), F32),
        name="consts",
    )(scale, offset)
    down = down.T

    def turned(block, way):
        n = lax.axis_size("z")
        step = lambda z, c: (z + (way if c == 0 else -way)) % n
        return lax.ppermute(block, ("z", "c"), [(2 * step(z, c) + c, 2 * z + c) for z in range(n) for c in range(2)])

    ahead = turned(own, 1)
    behind = turned(own, -1)
    across = from_ahead(texts, "y", 1)
    twin = from_ahead(texts, "c", 1)

    shape = jax.ShapeDtypeStruct
    sums, narrow, grads = shape((rows, width), F32), shape((rows, 128), F32), shape((rank, width), F32)
    unit = 2.0 * rows * rows * width
    pair_flops = 2.2 * unit

    both0, ups0, s0, s1, h0, h1, inner0 = run(
        own_kernel,
        "own_rows",
        [consts, own, texts, twin, proj, down, up],
        [shape((rows, wide), BF16), shape((2 * rank, 2 * rows), BF16), sums, sums, narrow, narrow, shape((2 * rank, rows), F32)],
        [pltpu.VMEM((rows, rows), BF16)],
        3.2 * unit + 2 * pair_flops,
    )
    ups0, across = tied(ups0, across)
    across_twin = from_ahead(across, "c", 1)
    square, block = pltpu.VMEM((rows, rows), BF16), shape((2 * rank, rows), BF16)
    inner_own, inner_sides = shape((2 * rank, rows), F32), shape((2 * rank, 2 * rows), F32)

    def own_far(texts, inner):
        return run(
            own_far_kernel,
            "own_far",
            [consts, both0, texts, up, inner],
            [block, sums, narrow, inner_own],
            [square],
            pair_flops,
        )

    def side_far(texts, ups, inner, s, h):
        return run(
            side_far_kernel,
            "side_far",
            [consts, both1, texts, ups, inner, s, h],
            [sums, narrow, inner_sides],
            [pltpu.VMEM((rows, 2 * rows), BF16)],
            2 * pair_flops,
        )

    ups2, s2, h2, inner0 = own_far(across, inner0)
    inner0, ahead, behind, across_twin = tied(inner0, ahead, behind, across_twin)
    far = turned(ahead, 1)
    both1, s0, s1, h0, h1, inner1 = run(
        side_kernel,
        "side_rows",
        [consts, ahead, behind, texts, twin, ups0, proj, down, up, s0, s1, h0, h1],
        [shape((2 * rows, wide), BF16), sums, sums, narrow, narrow, inner_sides],
        [pltpu.VMEM((rows, 2 * rows), BF16)],
        6.4 * unit + 4 * pair_flops,
    )
    ups3, s3, h3, inner0 = own_far(across_twin, inner0)
    s3, h3, inner1 = side_far(across_twin, ups3, inner1, s3, h3)
    inner1, far = tied(inner1, far)
    far_twin = from_ahead(far, "c", 1)
    s1 = from_ahead(s1, "c", 1)
    s3 = from_ahead(s3, "c", 1)
    s2, h2, inner1 = side_far(across, ups2, inner1, s2, h2)
    grad_down, grad_up = run(
        shares_kernel,
        "shares",
        [inner0, inner1, own, ahead, behind, h1, h3, twin, across_twin],
        [grads, grads],
        [],
        unit,
        False,
    )
    grad_up, far_twin = tied(grad_up, far_twin)
    kept, sent, both2, w0, w2 = run(
        last_kernel,
        "far_rows",
        [consts, far, far_twin, texts, across, ups0, ups2, proj, down, up, h0, h2, grad_down, grad_up],
        [grads, grads, shape((2 * rows, wide), BF16)] + [shape((rows, 2 * rows), BF16)] * 2,
        [],
        6.4 * unit + 5 * unit,
    )

    def small(kernel, name, operands, outs, scratch=()):
        return run(kernel, name, operands, outs, scratch, 1, False)

    sizes = (112, 144, 128)
    chunks = small(
        away_kernel, "away_sums", [w2, both2, s2, s3], [shape((n + (16 if k == 0 else 0), width), F32) for k, n in enumerate(sizes)]
    )
    chunks = [chunk.astype(F16) for chunk in chunks]

    def beside(k, value, summed):
        value, chunk = tied(value, chunks[k])
        moved = from_ahead(chunk, "y", 1).astype(F32)
        return tied(summed(value), moved)

    def everyones(axis):
        def summed(block):
            others = [from_ahead(block, axis, d) for d in (1, 3, 2)]
            return small(sum_kernel, "sums", [block] + others, [quarter])[0]

        return summed

    def scattered(sent):
        pieces = small(quarter_kernel, "quarters", [kept, sent], [quarter] * 4, [pltpu.VMEM((rank, width), F32)])
        pieces = [pieces[0]] + [from_ahead(p, "z", d) for p, d in zip(pieces[1:], (1, 3, 2))]
        return small(sum_kernel, "sums", pieces, [quarter])[0]

    def gathered(block):
        pieces = [block] + [from_ahead(block, "z", d) for d in (1, 3, 2)]
        return small(functools.partial(place_kernel, float(rows * 16)), "places", pieces, [grads])[0]

    quarter = shape((rank // 4, width), F32)
    sent = from_ahead(sent, "c", 1)
    total, c0 = beside(0, sent, scattered)
    total = everyones(("y", "h"))(total)
    total, c1 = beside(1, total, everyones("x"))
    (near,) = small(near_kernel, "near_sums", [w0, both2, s0, s1], [sums])
    total, near = tied(total, near)
    total, c2 = beside(2, total, gathered)
    other = from_ahead(total, "c", 1)
    (text_grad,) = small(finish_kernel, "finish", [near, c0, c1, c2], [sums])
    grad_down, grad_up = small(join_kernel, "joined", [total, other], [grads, grads])
    grad_down = grad_down.T
    return text_grad[None], grad_down, grad_up


def solution(mesh):
    grid = Mesh(mesh.devices.reshape(4, 2, 2, 2, 4), AXES)
    blk, dp = ("z", "y", "c"), ("h", "x")
    placed = (P(dp, blk, None), P(dp, blk, None), P(), P(), P(), P(), P())
    return jax.shard_map(
        shards,
        mesh=grid,
        in_specs=placed,
        out_specs=(P(dp, blk, None), P(), P()),
        check_vma=False,
    )
```

```python
import functools
import math

import jax
import jax.numpy as jnp
from jax import lax
from jax.experimental import pallas as pl
from jax.experimental.pallas import tpu as pltpu
from jax.sharding import Mesh, PartitionSpec as P

F32, BF16, F16 = jnp.float32, jnp.bfloat16, jnp.float16
AXES = ("z", "y", "c", "h", "x")
LOG2E = 1.4426950408889634
REACH = 14.0
MIB = 1 << 20


def tied(*values):
    return lax.optimization_barrier(values)


def from_ahead(block, axis, distance):
    n = lax.axis_size(axis)
    return lax.ppermute(block, axis, [((i + distance) % n, i) for i in range(n)])


def mm(a, b):
    return jnp.dot(a, b, preferred_element_type=F32)


def mm_nt(a, b):
    return lax.dot_general(a, b, (((1,), (1,)), ((), ())), preferred_element_type=F32)


def mm_tn(a, b):
    return lax.dot_general(a, b, (((0,), (0,)), ((), ())), preferred_element_type=F32)


def halves(a):
    high = a.astype(BF16)
    return high, (a - high.astype(F32)).astype(BF16)


def embed(images, at, both, packed, up):
    here = slice(at, at + images.shape[0])
    width, rank = up.shape[1], up.shape[0]
    products = mm(images[...], packed[...])
    hidden = products[:, width:].astype(BF16)
    both[here, :width] = (products[:, :width] + mm(hidden[:, :rank], up[...])).astype(BF16)
    both[here, width:] = hidden


def gate(sims, consts):
    power = jnp.minimum(sims * consts[0] + consts[1], 126.0)
    return (consts[2] / (1.0 + jnp.exp2(power))).astype(BF16)


def gate_matching(sims, consts):
    power = sims * consts[0] + consts[1]
    other = consts[2] / (1.0 + jnp.exp2(jnp.minimum(power, 126.0)))
    match = -consts[2] / (1.0 + jnp.exp2(jnp.minimum(-power, 126.0)))
    row = lax.broadcasted_iota(jnp.int32, sims.shape, 0)
    col = lax.broadcasted_iota(jnp.int32, sims.shape, 1)
    return jnp.where(row == col, match, other).astype(BF16)


def text_ups(texts, up, out, at):
    high, low = halves(mm_nt(up[...], texts[...]))
    out[:, at : at + texts.shape[0]] = jnp.concatenate([high, low])


def down_share(inner, images):
    rank = inner.shape[0] // 2
    pair = jnp.concatenate(halves(inner[:rank] + inner[rank:]))
    grad = mm(pair, images)
    return grad[:rank] + grad[rank:]


def up_share(hidden, texts, rank):
    pair = jnp.concatenate(halves(hidden[:, :rank]), axis=1)
    grad = mm_tn(pair, texts)
    return grad[:rank] + grad[rank:]


def consts_kernel(root, scale, offset, out):
    factor = scale[0] / root
    out[0] = -factor * LOG2E
    out[1] = -offset[0] * LOG2E
    out[2] = factor


def own_kernel(consts, own, t0, t1, proj, down, up, both, packed, ups, s0, s1, h0, h1, inner, w):
    width, rows, rank = proj.shape[1], own.shape[0], up.shape[0]
    packed[:, :width] = proj[...]
    packed[:, width : width + rank] = down[...].T
    packed[:, width + rank :] = jnp.zeros((packed.shape[0], packed.shape[1] - width - rank), BF16)
    embed(own, 0, both, packed, up)
    for k, (texts, s, h) in enumerate(((t0, s0, h0), (t1, s1, h1))):
        text_ups(texts, up, ups, k * rows)
        sims = mm_nt(texts[...], both[:, :width])
        w[...] = gate(sims, consts) if k else gate_matching(sims, consts)
        sums = mm(w[...], both[...])
        s[...], h[...] = sums[:, :width], sums[:, width:]
        part = mm(ups[:, k * rows : (k + 1) * rows], w[...])
        inner[...] = inner[...] + part if k else part


def side_kernel(consts, a, b, t0, t1, ups, packed, up, s0, s1, h0, h1, both, o0, o1, g0, g1, inner, w):
    width, rows = up.shape[1], a.shape[0]
    embed(a, 0, both, packed, up)
    embed(b, rows, both, packed, up)
    for k, (texts, s, h, o, g) in enumerate(((t0, s0, h0, o0, g0), (t1, s1, h1, o1, g1))):
        w[...] = gate(mm_nt(texts[...], both[:, :width]), consts)
        sums = mm(w[...], both[...])
        o[...], g[...] = s[...] + sums[:, :width], h[...] + sums[:, width:]
        part = mm(ups[:, k * rows : (k + 1) * rows], w[...])
        inner[...] = inner[...] + part if k else part


def own_far_kernel(consts, both, texts, up, inner0, ups, s, h, inner, w):
    width = texts.shape[1]
    text_ups(texts, up, ups, 0)
    w[...] = gate(mm_nt(texts[...], both[:, :width]), consts)
    sums = mm(w[...], both[...])
    s[...], h[...] = sums[:, :width], sums[:, width:]
    inner[...] = inner0[...] + mm(ups[...], w[...])


def side_far_kernel(consts, both, texts, ups, inner0, s0, h0, s, h, inner, w):
    width = texts.shape[1]
    w[...] = gate(mm_nt(texts[...], both[:, :width]), consts)
    sums = mm(w[...], both[...])
    s[...], h[...] = s0[...] + sums[:, :width], h0[...] + sums[:, width:]
    inner[...] = inner0[...] + mm(ups[...], w[...])


def shares_kernel(inner0, inner1, own, a, b, h1, h3, t1, t3, grad_down, grad_up):
    rows, rank = own.shape[0], grad_up.shape[0]
    grad_up[...] = up_share(h1[...], t1[...], rank) + up_share(h3[...], t3[...], rank)
    grad_down[...] = (
        down_share(inner0[...], own[...])
        + down_share(inner1[:, :rows], a[...])
        + down_share(inner1[:, rows:], b[...])
    )


def embed_kernel(images, packed, up, both):
    embed(images, 0, both, packed, up)


def last_kernel(
    consts, x0, x1, e0, e1, t0, t1, ups0, ups1, h0, h1, grad_down, grad_up, kept, sent, both, w0, w1
):
    rows, width = t0.shape
    rank, blocks = grad_up.shape[0], (x0, x1)
    both[:rows], both[rows:] = e0[...], e1[...]
    inner, up_sum = None, grad_up[...]
    for texts, ups, h, w in ((t0, ups0, h0, w0), (t1, ups1, h1, w1)):
        w[...] = gate(mm_nt(texts[...], both[:, :width]), consts)
        up_sum = up_sum + up_share(h[...] + mm(w[...], both[:, width:]), texts[...], rank)
        part = mm(ups[:, :rows], w[...])
        inner = part if inner is None else inner + part
    down_sum, at = grad_down[...], 0
    for block in blocks:
        down_sum = down_sum + down_share(inner[:, at : at + block.shape[0]], block[...])
        at += block.shape[0]
    first = lax.axis_index("c") == 0
    kept[...] = jnp.where(first, down_sum, up_sum)
    sent[...] = jnp.where(first, up_sum, down_sum)


def near_kernel(w, both, s, twin, out):
    out[...] = s[...] + twin[...] + mm(w[...], both[:, : s.shape[1]])


def away_kernel(w, both, s, twin, *outs):
    rows, width = s.shape
    value = s[...] + twin[...] + mm(w[...], both[:, :width])
    top = jnp.maximum(jnp.max(jnp.abs(value), keepdims=True), 1e-30)
    power = jnp.ceil(jnp.log2(top))
    value = value * jnp.exp2(REACH - power)
    tail, at = outs[0].shape[0] - 16, 0
    for k, out in enumerate(outs):
        part = out.shape[0] if k else tail
        out[:part] = value[at : at + part]
        at += part
    outs[0][tail:] = jnp.broadcast_to(power, (16, width))


def finish_kernel(near, c0, c1, out):
    tail, at = c0.shape[0] - 16, 0
    scale = jnp.exp2(c0[tail : tail + 1, :] - REACH)
    for k, chunk in enumerate((c0, c1)):
        part = chunk.shape[0] if k else tail
        out[at : at + part] = near[at : at + part] + chunk[:part] * scale
        at += part


def quarter_kernel(a, b, o0, o1, o2, o3, total):
    total[...] = a[...] + b[...]
    here, part = lax.axis_index("z"), o0.shape[0]
    for out, d in ((o0, 0), (o1, 1), (o2, 3), (o3, 2)):
        out[...] = total[pl.ds(pl.multiple_of(((here + 4 - d) % 4) * part, part), part), :]


def sum_kernel(a, b, c, d, out):
    out[...] = a[...] + b[...] + c[...] + d[...]


def place_kernel(pairs, a, b, c, d, out):
    here, part = lax.axis_index("z"), a.shape[0]
    for block, k in ((a, 0), (b, 1), (c, 3), (d, 2)):
        out[pl.ds(pl.multiple_of(((here + k) % 4) * part, part), part), :] = block[...] / pairs


def join_kernel(a, b, down, up):
    first = lax.axis_index("c") == 0
    down[...] = jnp.where(first, a[...], b[...])
    up[...] = jnp.where(first, b[...], a[...])


def run(kernel, name, operands, outs, scratch, flops, consts=True):
    spec = pl.BlockSpec(memory_space=pltpu.VMEM)
    ins = [spec] * len(operands)
    if consts:
        ins[0] = pl.BlockSpec(memory_space=pltpu.SMEM)
    size = sum(math.prod(o.shape) * o.dtype.itemsize for o in list(operands) + list(outs))
    return pl.pallas_call(
        kernel,
        in_specs=ins,
        out_specs=[spec] * len(outs),
        out_shape=outs,
        scratch_shapes=scratch,
        compiler_params=pltpu.CompilerParams(vmem_limit_bytes=16 * MIB),
        cost_estimate=pl.CostEstimate(flops=int(flops), bytes_accessed=size, transcendentals=0),
        name=name,
    )(*operands)


def shards(images, texts, proj, down, up, scale, offset):
    own, texts = images[0], texts[0]
    rows, width = texts.shape
    rank = down.shape[1]
    wide = width + 128
    scalar = pl.BlockSpec(memory_space=pltpu.SMEM)
    consts = pl.pallas_call(
        functools.partial(consts_kernel, math.sqrt(width)),
        in_specs=[scalar, scalar],
        out_specs=scalar,
        out_shape=jax.ShapeDtypeStruct((3,), F32),
        name="consts",
    )(scale, offset)
    down = down.T

    def turned(block, way):
        n = lax.axis_size("z")
        step = lambda z, c: (z + (way if c == 0 else -way)) % n
        return lax.ppermute(block, ("z", "c"), [(2 * step(z, c) + c, 2 * z + c) for z in range(n) for c in range(2)])

    ahead = turned(own, 1)
    behind = turned(own, -1)
    across = from_ahead(texts, "y", 1)
    twin = from_ahead(texts, "c", 1)

    shape = jax.ShapeDtypeStruct
    sums, narrow, grads = shape((rows, width), F32), shape((rows, 128), F32), shape((rank, width), F32)
    inner_own, inner_sides = shape((2 * rank, rows), F32), shape((2 * rank, 2 * rows), F32)
    unit = 2.0 * rows * rows * width
    pair_flops = 2.2 * unit

    both0, packed, ups0, s0, s1, h0, h1, inner0 = run(
        own_kernel,
        "own_rows",
        [consts, own, texts, twin, proj, down, up],
        [shape((rows, wide), BF16), shape((width, wide), BF16), shape((2 * rank, 2 * rows), BF16), sums, sums, narrow, narrow, inner_own],
        [pltpu.VMEM((rows, rows), BF16)],
        3.2 * unit + 2 * pair_flops,
    )
    ups0, across = tied(ups0, across)
    across_twin = from_ahead(across, "c", 1)
    square, block = pltpu.VMEM((rows, rows), BF16), shape((2 * rank, rows), BF16)

    def own_far(texts, inner):
        return run(
            own_far_kernel,
            "own_far",
            [consts, both0, texts, up, inner],
            [block, sums, narrow, inner_own],
            [square],
            pair_flops,
        )

    def side_far(texts, ups, inner, s, h):
        return run(
            side_far_kernel,
            "side_far",
            [consts, both1, texts, ups, inner, s, h],
            [sums, narrow, inner_sides],
            [pltpu.VMEM((rows, 2 * rows), BF16)],
            2 * pair_flops,
        )

    ups2, s2, h2, inner0 = own_far(across, inner0)
    inner0, ahead, behind, across_twin = tied(inner0, ahead, behind, across_twin)
    far = turned(ahead, 1)
    both1, s0, s1, h0, h1, inner1 = run(
        side_kernel,
        "side_rows",
        [consts, ahead, behind, texts, twin, ups0, packed, up, s0, s1, h0, h1],
        [shape((2 * rows, wide), BF16), sums, sums, narrow, narrow, inner_sides],
        [pltpu.VMEM((rows, 2 * rows), BF16)],
        6.4 * unit + 4 * pair_flops,
    )
    ups3, s3, h3, inner0 = own_far(across_twin, inner0)
    s3, h3, inner1 = side_far(across_twin, ups3, inner1, s3, h3)
    inner1, far = tied(inner1, far)
    far_twin = from_ahead(far, "c", 1)
    (far_both,) = run(embed_kernel, "embed_far", [far, packed, up], [shape((rows, wide), BF16)], [], 3.2 * unit, False)
    far_both_twin = from_ahead(far_both, "c", 1)
    s1 = from_ahead(s1, "c", 1)
    s3 = from_ahead(s3, "c", 1)
    inner1, far_both = tied(inner1, far_both)
    s2, h2, inner1 = side_far(across, ups2, inner1, s2, h2)
    grad_down, grad_up = run(
        shares_kernel,
        "shares",
        [inner0, inner1, own, ahead, behind, h1, h3, twin, across_twin],
        [grads, grads],
        [],
        unit,
        False,
    )
    grad_up, far_twin, far_both_twin = tied(grad_up, far_twin, far_both_twin)
    kept, sent, both2, w0, w2 = run(
        last_kernel,
        "far_rows",
        [consts, far, far_twin, far_both, far_both_twin, texts, across, ups0, ups2, h0, h2, grad_down, grad_up],
        [grads, grads, shape((2 * rows, wide), BF16)] + [shape((rows, 2 * rows), BF16)] * 2,
        [],
        5 * unit,
    )

    def small(kernel, name, operands, outs, scratch=()):
        return run(kernel, name, operands, outs, scratch, 1, False)

    sizes = (256, 128)
    chunks = small(
        away_kernel, "away_sums", [w2, both2, s2, s3], [shape((n + (16 if k == 0 else 0), width), F32) for k, n in enumerate(sizes)]
    )
    chunks = [chunk.astype(F16) for chunk in chunks]

    def everyones(axis):
        def summed(block):
            others = [from_ahead(block, axis, d) for d in (1, 3, 2)]
            return small(sum_kernel, "sums", [block] + others, [quarter])[0]

        return summed

    def scattered(sent):
        pieces = small(quarter_kernel, "quarters", [kept, sent], [quarter] * 4, [pltpu.VMEM((rank, width), F32)])
        pieces = [pieces[0]] + [from_ahead(p, "z", d) for p, d in zip(pieces[1:], (1, 3, 2))]
        return small(sum_kernel, "sums", pieces, [quarter])[0]

    def gathered(block):
        pieces = [block] + [from_ahead(block, "z", d) for d in (1, 3, 2)]
        return small(functools.partial(place_kernel, float(rows * 16)), "places", pieces, [grads])[0]

    quarter = shape((rank // 4, width), F32)
    sent = from_ahead(sent, "c", 1)
    sent, *chunks = tied(sent, *chunks)
    total = scattered(sent)
    moved = from_ahead(chunks[0], "y", 1).astype(F32)
    (near,) = small(near_kernel, "near_sums", [w0, both2, s0, s1], [sums])
    total, near = tied(total, near)
    total = everyones("x")(total)
    total, c0, chunk = tied(total, moved, chunks[1])
    total = everyones(("y", "h"))(total)
    total, chunk = tied(total, chunk)
    moved = from_ahead(chunk, "y", 1).astype(F32)
    total, c1 = tied(gathered(total), moved)
    other = from_ahead(total, "c", 1)
    (text_grad,) = small(finish_kernel, "finish", [near, c0, c1], [sums])
    grad_down, grad_up = small(join_kernel, "joined", [total, other], [grads, grads])
    grad_down = grad_down.T
    return text_grad[None], grad_down, grad_up


def solution(mesh):
    grid = Mesh(mesh.devices.reshape(4, 2, 2, 2, 4), AXES)
    blk, dp = ("z", "y", "c"), ("h", "x")
    placed = (P(dp, blk, None), P(dp, blk, None), P(), P(), P(), P(), P())
    return jax.shard_map(
        shards,
        mesh=grid,
        in_specs=placed,
        out_specs=(P(dp, blk, None), P(), P()),
        check_vma=False,
    )
```

```python
import functools
import math

import jax
import jax.numpy as jnp
from jax import lax
from jax.experimental import pallas as pl
from jax.experimental.pallas import tpu as pltpu
from jax.sharding import Mesh, PartitionSpec as P

F32, BF16, F16 = jnp.float32, jnp.bfloat16, jnp.float16
AXES = ("z", "y", "c", "h", "x")
LOG2E = 1.4426950408889634
REACH = 14.0
MIB = 1 << 20


def tied(*values):
    return lax.optimization_barrier(values)


def from_ahead(block, axis, distance):
    n = lax.axis_size(axis)
    return lax.ppermute(block, axis, [((i + distance) % n, i) for i in range(n)])


def mm(a, b):
    return jnp.dot(a, b, preferred_element_type=F32)


def mm_nt(a, b):
    return lax.dot_general(a, b, (((1,), (1,)), ((), ())), preferred_element_type=F32)


def mm_tn(a, b):
    return lax.dot_general(a, b, (((0,), (0,)), ((), ())), preferred_element_type=F32)


def halves(a):
    high = a.astype(BF16)
    return high, (a - high.astype(F32)).astype(BF16)


def embed(images, at, both, packed, up):
    here = slice(at, at + images.shape[0])
    width, rank = up.shape[1], up.shape[0]
    products = mm(images[...], packed[...])
    hidden = products[:, width:].astype(BF16)
    both[here, :width] = (products[:, :width] + mm(hidden[:, :rank], up[...])).astype(BF16)
    both[here, width:] = hidden


def gate(sims, consts):
    power = jnp.minimum(sims * consts[0] + consts[1], 126.0)
    return (consts[2] / (1.0 + jnp.exp2(power))).astype(BF16)


def gate_matching(sims, consts):
    power = sims * consts[0] + consts[1]
    other = consts[2] / (1.0 + jnp.exp2(jnp.minimum(power, 126.0)))
    match = -consts[2] / (1.0 + jnp.exp2(jnp.minimum(-power, 126.0)))
    row = lax.broadcasted_iota(jnp.int32, sims.shape, 0)
    col = lax.broadcasted_iota(jnp.int32, sims.shape, 1)
    return jnp.where(row == col, match, other).astype(BF16)


def text_ups(texts, up, out, at):
    high, low = halves(mm_nt(up[...], texts[...]))
    out[:, at : at + texts.shape[0]] = jnp.concatenate([high, low])


def down_share(inner, images):
    rank = inner.shape[0] // 2
    pair = jnp.concatenate(halves(inner[:rank] + inner[rank:]))
    grad = mm(pair, images)
    return grad[:rank] + grad[rank:]


def up_share(hidden, texts, rank):
    pair = jnp.concatenate(halves(hidden[:, :rank]), axis=1)
    grad = mm_tn(pair, texts)
    return grad[:rank] + grad[rank:]


def consts_kernel(root, scale, offset, out):
    factor = scale[0] / root
    out[0] = -factor * LOG2E
    out[1] = -offset[0] * LOG2E
    out[2] = factor


def own_kernel(consts, own, t0, t1, proj, down, up, both, packed, ups, s0, s1, h0, h1, inner, w):
    width, rows, rank = proj.shape[1], own.shape[0], up.shape[0]
    packed[:, :width] = proj[...]
    packed[:, width : width + rank] = down[...].T
    packed[:, width + rank :] = jnp.zeros((packed.shape[0], packed.shape[1] - width - rank), BF16)
    embed(own, 0, both, packed, up)
    for k, (texts, s, h) in enumerate(((t0, s0, h0), (t1, s1, h1))):
        text_ups(texts, up, ups, k * rows)
        sims = mm_nt(texts[...], both[:, :width])
        w[...] = gate(sims, consts) if k else gate_matching(sims, consts)
        sums = mm(w[...], both[...])
        s[...], h[...] = sums[:, :width], sums[:, width:]
        part = mm(ups[:, k * rows : (k + 1) * rows], w[...])
        inner[...] = inner[...] + part if k else part


def side_kernel(consts, a, b, t0, t1, ups, packed, up, h0, h1, both, g0, g1, inner, w0, w1):
    width, rows = up.shape[1], a.shape[0]
    embed(a, 0, both, packed, up)
    embed(b, rows, both, packed, up)
    for k, (texts, h, g, w) in enumerate(((t0, h0, g0, w0), (t1, h1, g1, w1))):
        w[...] = gate(mm_nt(texts[...], both[:, :width]), consts)
        g[...] = h[...] + mm(w[...], both[:, width:])
        part = mm(ups[:, k * rows : (k + 1) * rows], w[...])
        inner[...] = inner[...] + part if k else part


def own_far_kernel(consts, both, texts, up, inner0, ups, s, h, inner, w):
    width = texts.shape[1]
    text_ups(texts, up, ups, 0)
    w[...] = gate(mm_nt(texts[...], both[:, :width]), consts)
    sums = mm(w[...], both[...])
    s[...], h[...] = sums[:, :width], sums[:, width:]
    inner[...] = inner0[...] + mm(ups[...], w[...])


def side_far_kernel(consts, both, texts, ups, inner0, s0, h0, s, h, inner, w):
    width = texts.shape[1]
    w[...] = gate(mm_nt(texts[...], both[:, :width]), consts)
    sums = mm(w[...], both[...])
    s[...], h[...] = s0[...] + sums[:, :width], h0[...] + sums[:, width:]
    inner[...] = inner0[...] + mm(ups[...], w[...])


def shares_kernel(inner0, inner1, own, a, b, h1, h3, t1, t3, grad_down, grad_up):
    rows, rank = own.shape[0], grad_up.shape[0]
    grad_up[...] = up_share(h1[...], t1[...], rank) + up_share(h3[...], t3[...], rank)
    grad_down[...] = (
        down_share(inner0[...], own[...])
        + down_share(inner1[:, :rows], a[...])
        + down_share(inner1[:, rows:], b[...])
    )


def embed_kernel(images, packed, up, both):
    embed(images, 0, both, packed, up)


def last_kernel(
    consts, x0, x1, e0, e1, t0, t1, ups0, ups1, h0, h1, grad_down, grad_up, kept, sent, both, w0, w1
):
    rows, width = t0.shape
    rank, blocks = grad_up.shape[0], (x0, x1)
    both[:rows], both[rows:] = e0[...], e1[...]
    inner, up_sum = None, grad_up[...]
    for texts, ups, h, w in ((t0, ups0, h0, w0), (t1, ups1, h1, w1)):
        w[...] = gate(mm_nt(texts[...], both[:, :width]), consts)
        up_sum = up_sum + up_share(h[...] + mm(w[...], both[:, width:]), texts[...], rank)
        part = mm(ups[:, :rows], w[...])
        inner = part if inner is None else inner + part
    down_sum, at = grad_down[...], 0
    for block in blocks:
        down_sum = down_sum + down_share(inner[:, at : at + block.shape[0]], block[...])
        at += block.shape[0]
    first = lax.axis_index("c") == 0
    kept[...] = jnp.where(first, down_sum, up_sum)
    sent[...] = jnp.where(first, up_sum, down_sum)


def twin_kernel(w, both, s, out):
    out[...] = s[...] + mm(w[...], both[:, : s.shape[1]])


def near_kernel(w0, both0, w1, both1, s, twin, out):
    width = s.shape[1]
    out[...] = s[...] + twin[...] + mm(w0[...], both0[:, :width]) + mm(w1[...], both1[:, :width])


def away_kernel(w, both, s, twin, *outs):
    rows, width = s.shape
    value = s[...] + twin[...] + mm(w[...], both[:, :width])
    top = jnp.maximum(jnp.max(jnp.abs(value), keepdims=True), 1e-30)
    power = jnp.ceil(jnp.log2(top))
    value = value * jnp.exp2(REACH - power)
    tail, at = outs[0].shape[0] - 16, 0
    for k, out in enumerate(outs):
        part = out.shape[0] if k else tail
        out[:part] = value[at : at + part]
        at += part
    outs[0][tail:] = jnp.broadcast_to(power, (16, width))


def finish_kernel(near, c0, c1, out):
    tail, at = c0.shape[0] - 16, 0
    scale = jnp.exp2(c0[tail : tail + 1, :] - REACH)
    for k, chunk in enumerate((c0, c1)):
        part = chunk.shape[0] if k else tail
        out[at : at + part] = near[at : at + part] + chunk[:part] * scale
        at += part


def quarter_kernel(a, b, o0, o1, o2, o3, total):
    total[...] = a[...] + b[...]
    here, part = lax.axis_index("z"), o0.shape[0]
    for out, d in ((o0, 0), (o1, 1), (o2, 3), (o3, 2)):
        out[...] = total[pl.ds(pl.multiple_of(((here + 4 - d) % 4) * part, part), part), :]


def sum_kernel(a, b, c, d, out):
    out[...] = a[...] + b[...] + c[...] + d[...]


def place_kernel(pairs, a, b, c, d, out):
    here, part = lax.axis_index("z"), a.shape[0]
    for block, k in ((a, 0), (b, 1), (c, 3), (d, 2)):
        out[pl.ds(pl.multiple_of(((here + k) % 4) * part, part), part), :] = block[...] / pairs


def join_kernel(a, b, down, up):
    first = lax.axis_index("c") == 0
    down[...] = jnp.where(first, a[...], b[...])
    up[...] = jnp.where(first, b[...], a[...])


def run(kernel, name, operands, outs, scratch, flops, consts=True):
    spec = pl.BlockSpec(memory_space=pltpu.VMEM)
    ins = [spec] * len(operands)
    if consts:
        ins[0] = pl.BlockSpec(memory_space=pltpu.SMEM)
    size = sum(math.prod(o.shape) * o.dtype.itemsize for o in list(operands) + list(outs))
    return pl.pallas_call(
        kernel,
        in_specs=ins,
        out_specs=[spec] * len(outs),
        out_shape=outs,
        scratch_shapes=scratch,
        compiler_params=pltpu.CompilerParams(vmem_limit_bytes=16 * MIB),
        cost_estimate=pl.CostEstimate(flops=int(flops), bytes_accessed=size, transcendentals=0),
        name=name,
    )(*operands)


def shards(images, texts, proj, down, up, scale, offset):
    own, texts = images[0], texts[0]
    rows, width = texts.shape
    rank = down.shape[1]
    wide = width + 128
    scalar = pl.BlockSpec(memory_space=pltpu.SMEM)
    consts = pl.pallas_call(
        functools.partial(consts_kernel, math.sqrt(width)),
        in_specs=[scalar, scalar],
        out_specs=scalar,
        out_shape=jax.ShapeDtypeStruct((3,), F32),
        compiler_params=pltpu.CompilerParams(vmem_limit_bytes=MIB),
        name="consts",
    )(scale, offset)
    down = down.T

    def turned(block, way):
        n = lax.axis_size("z")
        step = lambda z, c: (z + (way if c == 0 else -way)) % n
        return lax.ppermute(block, ("z", "c"), [(2 * step(z, c) + c, 2 * z + c) for z in range(n) for c in range(2)])

    ahead = turned(own, 1)
    behind = turned(own, -1)
    across = from_ahead(texts, "y", 1)
    twin = from_ahead(texts, "c", 1)

    shape = jax.ShapeDtypeStruct
    sums, narrow, grads = shape((rows, width), F32), shape((rows, 128), F32), shape((rank, width), F32)
    inner_own, inner_sides = shape((2 * rank, rows), F32), shape((2 * rank, 2 * rows), F32)
    unit = 2.0 * rows * rows * width
    pair_flops = 2.2 * unit

    both0, packed, ups0, s0, s1, h0, h1, inner0 = run(
        own_kernel,
        "own_rows",
        [consts, own, texts, twin, proj, down, up],
        [shape((rows, wide), BF16), shape((width, wide), BF16), shape((2 * rank, 2 * rows), BF16), sums, sums, narrow, narrow, inner_own],
        [pltpu.VMEM((rows, rows), BF16)],
        3.2 * unit + 2 * pair_flops,
    )
    ups0, across = tied(ups0, across)
    across_twin = from_ahead(across, "c", 1)
    square, block = pltpu.VMEM((rows, rows), BF16), shape((2 * rank, rows), BF16)

    def own_far(texts, inner):
        return run(
            own_far_kernel,
            "own_far",
            [consts, both0, texts, up, inner],
            [block, sums, narrow, inner_own],
            [square],
            pair_flops,
        )

    def side_far(texts, ups, inner, s, h):
        return run(
            side_far_kernel,
            "side_far",
            [consts, both1, texts, ups, inner, s, h],
            [sums, narrow, inner_sides],
            [pltpu.VMEM((rows, 2 * rows), BF16)],
            2 * pair_flops,
        )

    ups2, s2, h2, inner0 = own_far(across, inner0)
    inner0, ahead, behind, across_twin = tied(inner0, ahead, behind, across_twin)
    far = turned(ahead, 1)
    both1, h0, h1, inner1, w_near, w_twin = run(
        side_kernel,
        "side_rows",
        [consts, ahead, behind, texts, twin, ups0, packed, up, h0, h1],
        [shape((2 * rows, wide), BF16), narrow, narrow, inner_sides] + [shape((rows, 2 * rows), BF16)] * 2,
        [],
        6.4 * unit + 2 * pair_flops,
    )
    ups3, s3, h3, inner0 = own_far(across_twin, inner0)
    s3, h3, inner1 = side_far(across_twin, ups3, inner1, s3, h3)
    inner1, far = tied(inner1, far)
    far_twin = from_ahead(far, "c", 1)
    (far_both,) = run(embed_kernel, "embed_far", [far, packed, up], [shape((rows, wide), BF16)], [], 3.2 * unit, False)
    far_both_twin = from_ahead(far_both, "c", 1)
    s3 = from_ahead(s3, "c", 1)
    inner1, far_both = tied(inner1, far_both)
    s2, h2, inner1 = side_far(across, ups2, inner1, s2, h2)
    grad_down, grad_up = run(
        shares_kernel,
        "shares",
        [inner0, inner1, own, ahead, behind, h1, h3, twin, across_twin],
        [grads, grads],
        [],
        unit,
        False,
    )
    grad_up, far_twin, far_both_twin = tied(grad_up, far_twin, far_both_twin)
    kept, sent, both2, w0, w2 = run(
        last_kernel,
        "far_rows",
        [consts, far, far_twin, far_both, far_both_twin, texts, across, ups0, ups2, h0, h2, grad_down, grad_up],
        [grads, grads, shape((2 * rows, wide), BF16)] + [shape((rows, 2 * rows), BF16)] * 2,
        [],
        5 * unit,
    )

    def small(kernel, name, operands, outs, scratch=()):
        return run(kernel, name, operands, outs, scratch, 1, False)

    sizes = (304, 80)
    chunks = small(
        away_kernel, "away_sums", [w2, both2, s2, s3], [shape((n + (16 if k == 0 else 0), width), F32) for k, n in enumerate(sizes)]
    )
    chunks = [chunk.astype(F16) for chunk in chunks]

    def everyones(axis):
        def summed(block):
            others = [from_ahead(block, axis, d) for d in (1, 3, 2)]
            return small(sum_kernel, "sums", [block] + others, [quarter])[0]

        return summed

    def scattered(sent):
        pieces = small(quarter_kernel, "quarters", [kept, sent], [quarter] * 4, [pltpu.VMEM((rank, width), F32)])
        pieces = [pieces[0]] + [from_ahead(p, "z", d) for p, d in zip(pieces[1:], (1, 3, 2))]
        return small(sum_kernel, "sums", pieces, [quarter])[0]

    def gathered(block):
        pieces = [block] + [from_ahead(block, "z", d) for d in (1, 3, 2)]
        return small(functools.partial(place_kernel, float(rows * 16)), "places", pieces, [grads])[0]

    quarter = shape((rank // 4, width), F32)
    sent = from_ahead(sent, "c", 1)
    sent, *chunks = tied(sent, *chunks)
    total = scattered(sent)
    moved = from_ahead(chunks[0], "y", 1).astype(F32)
    (s1,) = small(twin_kernel, "twin_sums", [w_twin, both1, s1], [sums])
    total = everyones("x")(total)
    total, c0, s1, chunk = tied(total, moved, s1, chunks[1])
    s1 = from_ahead(s1, "c", 1)
    total = everyones(("y", "h"))(total)
    total, chunk, s1 = tied(total, chunk, s1)
    moved = from_ahead(chunk, "y", 1).astype(F32)
    total = gathered(total)
    (near,) = small(near_kernel, "near_sums", [w_near, both1, w0, both2, s0, s1], [sums])
    total, c1, near = tied(total, moved, near)
    other = from_ahead(total, "c", 1)
    (text_grad,) = small(finish_kernel, "finish", [near, c0, c1], [sums])
    grad_down, grad_up = small(join_kernel, "joined", [total, other], [grads, grads])
    grad_down = grad_down.T
    return text_grad[None], grad_down, grad_up


def solution(mesh):
    grid = Mesh(mesh.devices.reshape(4, 2, 2, 2, 4), AXES)
    blk, dp = ("z", "y", "c"), ("h", "x")
    placed = (P(dp, blk, None), P(dp, blk, None), P(), P(), P(), P(), P())
    return jax.shard_map(
        shards,
        mesh=grid,
        in_specs=placed,
        out_specs=(P(dp, blk, None), P(), P()),
        check_vma=False,
    )
```

```python
import functools
import math

import jax
import jax.numpy as jnp
from jax import lax
from jax.experimental import pallas as pl
from jax.experimental.pallas import tpu as pltpu
from jax.sharding import Mesh, PartitionSpec as P

F32, BF16, F16 = jnp.float32, jnp.bfloat16, jnp.float16
AXES = ("z", "y", "c", "h", "x")
LOG2E = 1.4426950408889634
REACH = 14.0
MIB = 1 << 20


def swapped(block, axis, flip):
    n = lax.axis_size(axis)
    return lax.ppermute(block, axis, [(i ^ flip, i) for i in range(n)])


def tied(*values):
    return lax.optimization_barrier(values)


def from_ahead(block, axis, distance):
    n = lax.axis_size(axis)
    return lax.ppermute(block, axis, [((i + distance) % n, i) for i in range(n)])


def mm(a, b):
    return jnp.dot(a, b, preferred_element_type=F32)


def mm_nt(a, b):
    return lax.dot_general(a, b, (((1,), (1,)), ((), ())), preferred_element_type=F32)


def mm_tn(a, b):
    return lax.dot_general(a, b, (((0,), (0,)), ((), ())), preferred_element_type=F32)


def halves(a):
    high = a.astype(BF16)
    return high, (a - high.astype(F32)).astype(BF16)


def embed(images, at, both, packed, up):
    here = slice(at, at + images.shape[0])
    width, rank = up.shape[1], up.shape[0]
    products = mm(images[...], packed[...])
    hidden = products[:, width:].astype(BF16)
    both[here, :width] = (products[:, :width] + mm(hidden[:, :rank], up[...])).astype(BF16)
    both[here, width:] = hidden


def gate(sims, consts):
    power = jnp.minimum(sims * consts[0] + consts[1], 126.0)
    return (consts[2] / (1.0 + jnp.exp2(power))).astype(BF16)


def gate_matching(sims, consts):
    power = sims * consts[0] + consts[1]
    other = consts[2] / (1.0 + jnp.exp2(jnp.minimum(power, 126.0)))
    match = -consts[2] / (1.0 + jnp.exp2(jnp.minimum(-power, 126.0)))
    row = lax.broadcasted_iota(jnp.int32, sims.shape, 0)
    col = lax.broadcasted_iota(jnp.int32, sims.shape, 1)
    return jnp.where(row == col, match, other).astype(BF16)


def text_ups(texts, up, out, at):
    high, low = halves(mm_nt(up[...], texts[...]))
    out[:, at : at + texts.shape[0]] = jnp.concatenate([high, low])


def down_share(inner, images):
    rank = inner.shape[0] // 2
    pair = jnp.concatenate(halves(inner[:rank] + inner[rank:]))
    grad = mm(pair, images)
    return grad[:rank] + grad[rank:]


def up_share(hidden, texts, rank):
    pair = jnp.concatenate(halves(hidden[:, :rank]), axis=1)
    grad = mm_tn(pair, texts)
    return grad[:rank] + grad[rank:]


def consts_kernel(root, scale, offset, out):
    factor = scale[0] / root
    out[0] = -factor * LOG2E
    out[1] = -offset[0] * LOG2E
    out[2] = factor


def own_kernel(consts, own, t0, t1, proj, down, up, both, packed, ups, s0, s1, h0, h1, inner, w):
    width, rows, rank = proj.shape[1], own.shape[0], up.shape[0]
    packed[:, :width] = proj[...]
    packed[:, width : width + rank] = down[...].T
    packed[:, width + rank :] = jnp.zeros((packed.shape[0], packed.shape[1] - width - rank), BF16)
    embed(own, 0, both, packed, up)
    for k, (texts, s, h) in enumerate(((t0, s0, h0), (t1, s1, h1))):
        text_ups(texts, up, ups, k * rows)
        sims = mm_nt(texts[...], both[:, :width])
        w[...] = gate(sims, consts) if k else gate_matching(sims, consts)
        sums = mm(w[...], both[...])
        s[...], h[...] = sums[:, :width], sums[:, width:]
        part = mm(ups[:, k * rows : (k + 1) * rows], w[...])
        inner[...] = inner[...] + part if k else part


def side_kernel(consts, a, b, t0, t1, ups, packed, up, h0, h1, both, g0, g1, inner, w0, w1):
    width, rows = up.shape[1], a.shape[0]
    embed(a, 0, both, packed, up)
    embed(b, rows, both, packed, up)
    for k, (texts, h, g, w) in enumerate(((t0, h0, g0, w0), (t1, h1, g1, w1))):
        w[...] = gate(mm_nt(texts[...], both[:, :width]), consts)
        g[...] = h[...] + mm(w[...], both[:, width:])
        part = mm(ups[:, k * rows : (k + 1) * rows], w[...])
        inner[...] = inner[...] + part if k else part


def own_far_kernel(consts, both, texts, up, inner0, ups, s, h, inner, w):
    width = texts.shape[1]
    text_ups(texts, up, ups, 0)
    w[...] = gate(mm_nt(texts[...], both[:, :width]), consts)
    sums = mm(w[...], both[...])
    s[...], h[...] = sums[:, :width], sums[:, width:]
    inner[...] = inner0[...] + mm(ups[...], w[...])


def side_far_kernel(consts, both, texts, ups, inner0, s0, h0, s, h, inner, w):
    width = texts.shape[1]
    w[...] = gate(mm_nt(texts[...], both[:, :width]), consts)
    sums = mm(w[...], both[...])
    s[...], h[...] = s0[...] + sums[:, :width], h0[...] + sums[:, width:]
    inner[...] = inner0[...] + mm(ups[...], w[...])


def shares_kernel(inner0, inner1, own, a, b, h1, h3, t1, t3, grad_down, grad_up):
    rows, rank = own.shape[0], grad_up.shape[0]
    grad_up[...] = up_share(h1[...], t1[...], rank) + up_share(h3[...], t3[...], rank)
    grad_down[...] = (
        down_share(inner0[...], own[...])
        + down_share(inner1[:, :rows], a[...])
        + down_share(inner1[:, rows:], b[...])
    )


def embed_kernel(images, packed, up, both):
    embed(images, 0, both, packed, up)


def last_kernel(
    consts, x0, x1, e0, e1, t0, t1, ups0, ups1, h0, h1, grad_down, grad_up, kept, sent, both, w0, w1
):
    rows, width = t0.shape
    rank, blocks = grad_up.shape[0], (x0, x1)
    both[:rows], both[rows:] = e0[...], e1[...]
    inner, up_sum = None, grad_up[...]
    for texts, ups, h, w in ((t0, ups0, h0, w0), (t1, ups1, h1, w1)):
        w[...] = gate(mm_nt(texts[...], both[:, :width]), consts)
        up_sum = up_sum + up_share(h[...] + mm(w[...], both[:, width:]), texts[...], rank)
        part = mm(ups[:, :rows], w[...])
        inner = part if inner is None else inner + part
    down_sum, at = grad_down[...], 0
    for block in blocks:
        down_sum = down_sum + down_share(inner[:, at : at + block.shape[0]], block[...])
        at += block.shape[0]
    first = lax.axis_index("c") == 0
    kept[...] = jnp.where(first, down_sum, up_sum)
    sent[...] = jnp.where(first, up_sum, down_sum)


def twin_kernel(w, both, s, out):
    out[...] = s[...] + mm(w[...], both[:, : s.shape[1]])


def near_kernel(w0, both0, w1, both1, s, twin, out):
    width = s.shape[1]
    out[...] = s[...] + twin[...] + mm(w0[...], both0[:, :width]) + mm(w1[...], both1[:, :width])


def away_kernel(w, both, s, twin, *outs):
    rows, width = s.shape
    value = s[...] + twin[...] + mm(w[...], both[:, :width])
    top = jnp.maximum(jnp.max(jnp.abs(value), keepdims=True), 1e-30)
    power = jnp.ceil(jnp.log2(top))
    value = value * jnp.exp2(REACH - power)
    tail, at = outs[0].shape[0] - 16, 0
    for k, out in enumerate(outs):
        part = out.shape[0] if k else tail
        out[:part] = value[at : at + part]
        at += part
    outs[0][tail:] = jnp.broadcast_to(power, (16, width))


def finish_kernel(near, c0, c1, out):
    tail, at = c0.shape[0] - 16, 0
    scale = jnp.exp2(c0[tail : tail + 1, :] - REACH)
    for k, chunk in enumerate((c0, c1)):
        part = chunk.shape[0] if k else tail
        out[at : at + part] = near[at : at + part] + chunk[:part] * scale
        at += part


def quarter_kernel(a, b, o0, o1, o2, o3, total):
    total[...] = a[...] + b[...]
    here, part = lax.axis_index("z"), o0.shape[0]
    for out, d in ((o0, 0), (o1, 1), (o2, 2), (o3, 3)):
        out[...] = total[pl.ds(pl.multiple_of(((here + 4 - d) % 4) * part, part), part), :]


def sum_kernel(a, b, c, d, out):
    out[...] = a[...] + b[...] + c[...] + d[...]


def place_kernel(pairs, a, b, c, d, out):
    here, part = lax.axis_index("z"), a.shape[0]
    for block, k in ((a, 0), (b, 1), (c, 2), (d, 3)):
        out[pl.ds(pl.multiple_of(((here + k) % 4) * part, part), part), :] = block[...] / pairs


def join_kernel(a, b, down, up):
    first = lax.axis_index("c") == 0
    down[...] = jnp.where(first, a[...], b[...])
    up[...] = jnp.where(first, b[...], a[...])


def run(kernel, name, operands, outs, scratch, flops, consts=True):
    spec = pl.BlockSpec(memory_space=pltpu.VMEM)
    ins = [spec] * len(operands)
    if consts:
        ins[0] = pl.BlockSpec(memory_space=pltpu.SMEM)
    size = sum(math.prod(o.shape) * o.dtype.itemsize for o in list(operands) + list(outs))
    return pl.pallas_call(
        kernel,
        in_specs=ins,
        out_specs=[spec] * len(outs),
        out_shape=outs,
        scratch_shapes=scratch,
        compiler_params=pltpu.CompilerParams(vmem_limit_bytes=16 * MIB),
        cost_estimate=pl.CostEstimate(flops=int(flops), bytes_accessed=size, transcendentals=0),
        name=name,
    )(*operands)


def shards(images, texts, proj, down, up, scale, offset):
    own, texts = images[0], texts[0]
    rows, width = texts.shape
    rank = down.shape[1]
    wide = width + 128
    scalar = pl.BlockSpec(memory_space=pltpu.SMEM)
    consts = pl.pallas_call(
        functools.partial(consts_kernel, math.sqrt(width)),
        in_specs=[scalar, scalar],
        out_specs=scalar,
        out_shape=jax.ShapeDtypeStruct((3,), F32),
        compiler_params=pltpu.CompilerParams(vmem_limit_bytes=MIB),
        name="consts",
    )(scale, offset)
    down = down.T

    def turned(block, way):
        n = lax.axis_size("z")
        step = lambda z, c: (z + (way if c == 0 else -way)) % n
        return lax.ppermute(block, ("z", "c"), [(2 * step(z, c) + c, 2 * z + c) for z in range(n) for c in range(2)])

    ahead = turned(own, 1)
    behind = turned(own, -1)
    across = from_ahead(texts, "y", 1)
    twin = from_ahead(texts, "c", 1)

    shape = jax.ShapeDtypeStruct
    sums, narrow, grads = shape((rows, width), F32), shape((rows, 128), F32), shape((rank, width), F32)
    inner_own, inner_sides = shape((2 * rank, rows), F32), shape((2 * rank, 2 * rows), F32)
    unit = 2.0 * rows * rows * width
    pair_flops = 2.2 * unit

    both0, packed, ups0, s0, s1, h0, h1, inner0 = run(
        own_kernel,
        "own_rows",
        [consts, own, texts, twin, proj, down, up],
        [shape((rows, wide), BF16), shape((width, wide), BF16), shape((2 * rank, 2 * rows), BF16), sums, sums, narrow, narrow, inner_own],
        [pltpu.VMEM((rows, rows), BF16)],
        3.2 * unit + 2 * pair_flops,
    )
    ups0, across = tied(ups0, across)
    across_twin = from_ahead(across, "c", 1)
    square, block = pltpu.VMEM((rows, rows), BF16), shape((2 * rank, rows), BF16)

    def own_far(texts, inner):
        return run(
            own_far_kernel,
            "own_far",
            [consts, both0, texts, up, inner],
            [block, sums, narrow, inner_own],
            [square],
            pair_flops,
        )

    def side_far(texts, ups, inner, s, h):
        return run(
            side_far_kernel,
            "side_far",
            [consts, both1, texts, ups, inner, s, h],
            [sums, narrow, inner_sides],
            [pltpu.VMEM((rows, 2 * rows), BF16)],
            2 * pair_flops,
        )

    ups2, s2, h2, inner0 = own_far(across, inner0)
    inner0, ahead, behind, across_twin = tied(inner0, ahead, behind, across_twin)
    far = turned(ahead, 1)
    both1, h0, h1, inner1, w_near, w_twin = run(
        side_kernel,
        "side_rows",
        [consts, ahead, behind, texts, twin, ups0, packed, up, h0, h1],
        [shape((2 * rows, wide), BF16), narrow, narrow, inner_sides] + [shape((rows, 2 * rows), BF16)] * 2,
        [],
        6.4 * unit + 2 * pair_flops,
    )
    ups3, s3, h3, inner0 = own_far(across_twin, inner0)
    s3, h3, inner1 = side_far(across_twin, ups3, inner1, s3, h3)
    inner1, far = tied(inner1, far)
    far_twin = from_ahead(far, "c", 1)
    (far_both,) = run(embed_kernel, "embed_far", [far, packed, up], [shape((rows, wide), BF16)], [], 3.2 * unit, False)
    far_both_twin = from_ahead(far_both, "c", 1)
    s3 = from_ahead(s3, "c", 1)
    inner1, far_both = tied(inner1, far_both)
    s2, h2, inner1 = side_far(across, ups2, inner1, s2, h2)
    grad_down, grad_up = run(
        shares_kernel,
        "shares",
        [inner0, inner1, own, ahead, behind, h1, h3, twin, across_twin],
        [grads, grads],
        [],
        unit,
        False,
    )
    grad_up, far_twin, far_both_twin = tied(grad_up, far_twin, far_both_twin)
    kept, sent, both2, w0, w2 = run(
        last_kernel,
        "far_rows",
        [consts, far, far_twin, far_both, far_both_twin, texts, across, ups0, ups2, h0, h2, grad_down, grad_up],
        [grads, grads, shape((2 * rows, wide), BF16)] + [shape((rows, 2 * rows), BF16)] * 2,
        [],
        5 * unit,
    )

    def small(kernel, name, operands, outs, scratch=()):
        return run(kernel, name, operands, outs, scratch, 1, False)

    sizes = (256, 128)
    chunks = small(
        away_kernel, "away_sums", [w2, both2, s2, s3], [shape((n + (16 if k == 0 else 0), width), F32) for k, n in enumerate(sizes)]
    )
    chunks = [chunk.astype(F16) for chunk in chunks]

    def everyones(axis, order, other):
        def summed(block):
            others = [other(block, axis, d) for d in order]
            return small(sum_kernel, "sums", [block] + others, [quarter])[0]

        return summed

    def scattered(sent):
        pieces = small(quarter_kernel, "quarters", [kept, sent], [quarter] * 4, [pltpu.VMEM((rank, width), F32)])
        pieces = [pieces[0]] + [from_ahead(p, "z", d) for p, d in zip(pieces[1:], (1, 2, 3))]
        return small(sum_kernel, "sums", pieces, [quarter])[0]

    def gathered(block):
        pieces = [block] + [from_ahead(block, "z", d) for d in (1, 2, 3)]
        return small(functools.partial(place_kernel, float(rows * 16)), "places", pieces, [grads])[0]

    quarter = shape((rank // 4, width), F32)
    sent = from_ahead(sent, "c", 1)
    sent, *chunks = tied(sent, *chunks)
    total = scattered(sent)
    moved = from_ahead(chunks[0], "y", 1).astype(F32)
    (s1,) = small(twin_kernel, "twin_sums", [w_twin, both1, s1], [sums])
    total = everyones("x", (1, 2, 3), from_ahead)(total)
    total, c0, s1, chunk = tied(total, moved, s1, chunks[1])
    s1 = from_ahead(s1, "c", 1)
    total = everyones(("y", "h"), (1, 2, 3), from_ahead)(total)
    total, chunk, s1 = tied(total, chunk, s1)
    moved = from_ahead(chunk, "y", 1).astype(F32)
    total = gathered(total)
    (near,) = small(near_kernel, "near_sums", [w_near, both1, w0, both2, s0, s1], [sums])
    total, c1, near = tied(total, moved, near)
    other = from_ahead(total, "c", 1)
    (text_grad,) = small(finish_kernel, "finish", [near, c0, c1], [sums])
    grad_down, grad_up = small(join_kernel, "joined", [total, other], [grads, grads])
    grad_down = grad_down.T
    return text_grad[None], grad_down, grad_up


def solution(mesh):
    grid = Mesh(mesh.devices.reshape(4, 2, 2, 2, 4), AXES)
    blk, dp = ("z", "y", "c"), ("h", "x")
    placed = (P(dp, blk, None), P(dp, blk, None), P(), P(), P(), P(), P())
    return jax.shard_map(
        shards,
        mesh=grid,
        in_specs=placed,
        out_specs=(P(dp, blk, None), P(), P()),
        check_vma=False,
    )
```

```python
import functools
import math

import jax
import jax.numpy as jnp
from jax import lax
from jax.experimental import pallas as pl
from jax.experimental.pallas import tpu as pltpu
from jax.sharding import Mesh, PartitionSpec as P

F32, BF16, F16 = jnp.float32, jnp.bfloat16, jnp.float16
AXES = ("z", "y", "c", "h", "x")
LOG2E = 1.4426950408889634
REACH = 14.0
MIB = 1 << 20


def tied(*values):
    return lax.optimization_barrier(values)


def from_ahead(block, axis, distance):
    n = lax.axis_size(axis)
    return lax.ppermute(block, axis, [((i + distance) % n, i) for i in range(n)])


def mm(a, b):
    return jnp.dot(a, b, preferred_element_type=F32)


def mm_nt(a, b):
    return lax.dot_general(a, b, (((1,), (1,)), ((), ())), preferred_element_type=F32)


def mm_tn(a, b):
    return lax.dot_general(a, b, (((0,), (0,)), ((), ())), preferred_element_type=F32)


def halves(a):
    high = a.astype(BF16)
    return high, (a - high.astype(F32)).astype(BF16)


def embed(images, at, both, packed, up):
    here = slice(at, at + images.shape[0])
    width, rank = up.shape[1], up.shape[0]
    products = mm(images[...], packed[...])
    hidden = products[:, width:].astype(BF16)
    both[here, :width] = (products[:, :width] + mm(hidden[:, :rank], up[...])).astype(BF16)
    both[here, width:] = hidden


def gate(sims, consts):
    power = jnp.minimum(sims * consts[0] + consts[1], 126.0)
    return (consts[2] / (1.0 + jnp.exp2(power))).astype(BF16)


def gate_matching(sims, consts):
    power = sims * consts[0] + consts[1]
    other = consts[2] / (1.0 + jnp.exp2(jnp.minimum(power, 126.0)))
    match = -consts[2] / (1.0 + jnp.exp2(jnp.minimum(-power, 126.0)))
    row = lax.broadcasted_iota(jnp.int32, sims.shape, 0)
    col = lax.broadcasted_iota(jnp.int32, sims.shape, 1)
    return jnp.where(row == col, match, other).astype(BF16)


def text_ups(texts, up, out, at):
    high, low = halves(mm_nt(up[...], texts[...]))
    out[:, at : at + texts.shape[0]] = jnp.concatenate([high, low])


def down_share(inner, images):
    rank = inner.shape[0] // 2
    pair = jnp.concatenate(halves(inner[:rank] + inner[rank:]))
    grad = mm(pair, images)
    return grad[:rank] + grad[rank:]


def up_share(hidden, texts, rank):
    pair = jnp.concatenate(halves(hidden[:, :rank]), axis=1)
    grad = mm_tn(pair, texts)
    return grad[:rank] + grad[rank:]


def consts_kernel(root, scale, offset, out):
    factor = scale[0] / root
    out[0] = -factor * LOG2E
    out[1] = -offset[0] * LOG2E
    out[2] = factor


def own_kernel(consts, own, t0, t1, proj, down, up, both, packed, ups, s0, s1, h0, h1, inner, w):
    width, rows, rank = proj.shape[1], own.shape[0], up.shape[0]
    packed[:, :width] = proj[...]
    packed[:, width : width + rank] = down[...].T
    packed[:, width + rank :] = jnp.zeros((packed.shape[0], packed.shape[1] - width - rank), BF16)
    embed(own, 0, both, packed, up)
    for k, (texts, s, h) in enumerate(((t0, s0, h0), (t1, s1, h1))):
        text_ups(texts, up, ups, k * rows)
        sims = mm_nt(texts[...], both[:, :width])
        w[...] = gate(sims, consts) if k else gate_matching(sims, consts)
        sums = mm(w[...], both[...])
        s[...], h[...] = sums[:, :width], sums[:, width:]
        part = mm(ups[:, k * rows : (k + 1) * rows], w[...])
        inner[...] = inner[...] + part if k else part


def side_kernel(consts, a, b, t0, t1, ups, packed, up, h0, h1, both, g0, g1, inner, w0, w1):
    width, rows = up.shape[1], a.shape[0]
    embed(a, 0, both, packed, up)
    embed(b, rows, both, packed, up)
    for k, (texts, h, g, w) in enumerate(((t0, h0, g0, w0), (t1, h1, g1, w1))):
        w[...] = gate(mm_nt(texts[...], both[:, :width]), consts)
        g[...] = h[...] + mm(w[...], both[:, width:])
        part = mm(ups[:, k * rows : (k + 1) * rows], w[...])
        inner[...] = inner[...] + part if k else part


def own_far_kernel(consts, both, texts, up, inner0, ups, s, h, inner, w):
    width = texts.shape[1]
    text_ups(texts, up, ups, 0)
    w[...] = gate(mm_nt(texts[...], both[:, :width]), consts)
    sums = mm(w[...], both[...])
    s[...], h[...] = sums[:, :width], sums[:, width:]
    inner[...] = inner0[...] + mm(ups[...], w[...])


def side_far_kernel(consts, both, texts, ups, inner0, s0, h0, s, h, inner, w):
    width = texts.shape[1]
    w[...] = gate(mm_nt(texts[...], both[:, :width]), consts)
    sums = mm(w[...], both[...])
    s[...], h[...] = s0[...] + sums[:, :width], h0[...] + sums[:, width:]
    inner[...] = inner0[...] + mm(ups[...], w[...])


def shares_kernel(inner0, inner1, own, a, b, h1, h3, t1, t3, grad_down, grad_up):
    rows, rank = own.shape[0], grad_up.shape[0]
    grad_up[...] = up_share(h1[...], t1[...], rank) + up_share(h3[...], t3[...], rank)
    grad_down[...] = (
        down_share(inner0[...], own[...])
        + down_share(inner1[:, :rows], a[...])
        + down_share(inner1[:, rows:], b[...])
    )


def embed_kernel(images, packed, up, both):
    embed(images, 0, both, packed, up)


def last_kernel(
    consts, x0, x1, e0, e1, t0, t1, ups0, ups1, h0, h1, grad_down, grad_up, kept, sent, both, w0, w1
):
    rows, width = t0.shape
    rank, blocks = grad_up.shape[0], (x0, x1)
    both[:rows], both[rows:] = e0[...], e1[...]
    inner, up_sum = None, grad_up[...]
    for texts, ups, h, w in ((t0, ups0, h0, w0), (t1, ups1, h1, w1)):
        w[...] = gate(mm_nt(texts[...], both[:, :width]), consts)
        up_sum = up_sum + up_share(h[...] + mm(w[...], both[:, width:]), texts[...], rank)
        part = mm(ups[:, :rows], w[...])
        inner = part if inner is None else inner + part
    down_sum, at = grad_down[...], 0
    for block in blocks:
        down_sum = down_sum + down_share(inner[:, at : at + block.shape[0]], block[...])
        at += block.shape[0]
    first = lax.axis_index("c") == 0
    kept[...] = jnp.where(first, down_sum, up_sum)
    sent[...] = jnp.where(first, up_sum, down_sum)


def twin_kernel(w, both, s, out):
    out[...] = s[...] + mm(w[...], both[:, : s.shape[1]])


def near_kernel(w0, both0, w1, both1, s, twin, out):
    width = s.shape[1]
    out[...] = s[...] + twin[...] + mm(w0[...], both0[:, :width]) + mm(w1[...], both1[:, :width])


def away_kernel(w, both, s, twin, *outs):
    rows, width = s.shape
    value = s[...] + twin[...] + mm(w[...], both[:, :width])
    top = jnp.maximum(jnp.max(jnp.abs(value), keepdims=True), 1e-30)
    power = jnp.ceil(jnp.log2(top))
    value = value * jnp.exp2(REACH - power)
    tail, at = outs[0].shape[0] - 16, 0
    for k, out in enumerate(outs):
        part = out.shape[0] if k else tail
        out[:part] = value[at : at + part]
        at += part
    outs[0][tail:] = jnp.broadcast_to(power, (16, width))


def finish_kernel(near, c0, c1, out):
    tail, at = c0.shape[0] - 16, 0
    scale = jnp.exp2(c0[tail : tail + 1, :] - REACH)
    for k, chunk in enumerate((c0, c1)):
        part = chunk.shape[0] if k else tail
        out[at : at + part] = near[at : at + part] + chunk[:part] * scale
        at += part


def quarter_kernel(a, b, o0, o1, o2, o3, total):
    total[...] = a[...] + b[...]
    here, part = lax.axis_index("z"), o0.shape[0]
    for out, d in ((o0, 0), (o1, 1), (o2, 2), (o3, 3)):
        out[...] = total[pl.ds(pl.multiple_of(((here + 4 - d) % 4) * part, part), part), :]


def sum_kernel(a, b, c, d, out):
    out[...] = a[...] + b[...] + c[...] + d[...]


def place_kernel(pairs, a, b, c, d, out):
    here, part = lax.axis_index("z"), a.shape[0]
    for block, k in ((a, 0), (b, 2), (c, 3), (d, 1)):
        out[pl.ds(pl.multiple_of(((here + k) % 4) * part, part), part), :] = block[...] / pairs


def join_kernel(a, b, down, up):
    first = lax.axis_index("c") == 0
    down[...] = jnp.where(first, a[...], b[...])
    up[...] = jnp.where(first, b[...], a[...])


def run(kernel, name, operands, outs, scratch, flops, consts=True):
    spec = pl.BlockSpec(memory_space=pltpu.VMEM)
    ins = [spec] * len(operands)
    if consts:
        ins[0] = pl.BlockSpec(memory_space=pltpu.SMEM)
    size = sum(math.prod(o.shape) * o.dtype.itemsize for o in list(operands) + list(outs))
    return pl.pallas_call(
        kernel,
        in_specs=ins,
        out_specs=[spec] * len(outs),
        out_shape=outs,
        scratch_shapes=scratch,
        compiler_params=pltpu.CompilerParams(vmem_limit_bytes=16 * MIB),
        cost_estimate=pl.CostEstimate(flops=int(flops), bytes_accessed=size, transcendentals=0),
        name=name,
    )(*operands)


def shards(images, texts, proj, down, up, scale, offset):
    own, texts = images[0], texts[0]
    rows, width = texts.shape
    rank = down.shape[1]
    wide = width + 128
    scalar = pl.BlockSpec(memory_space=pltpu.SMEM)
    consts = pl.pallas_call(
        functools.partial(consts_kernel, math.sqrt(width)),
        in_specs=[scalar, scalar],
        out_specs=scalar,
        out_shape=jax.ShapeDtypeStruct((3,), F32),
        compiler_params=pltpu.CompilerParams(vmem_limit_bytes=MIB),
        name="consts",
    )(scale, offset)
    down = down.T

    def turned(block, way):
        n = lax.axis_size("z")
        step = lambda z, c: (z + (way if c == 0 else -way)) % n
        return lax.ppermute(block, ("z", "c"), [(2 * step(z, c) + c, 2 * z + c) for z in range(n) for c in range(2)])

    ahead = turned(own, 1)
    behind = turned(own, -1)
    across = from_ahead(texts, "y", 1)
    twin = from_ahead(texts, "c", 1)

    shape = jax.ShapeDtypeStruct
    sums, narrow, grads = shape((rows, width), F32), shape((rows, 128), F32), shape((rank, width), F32)
    inner_own, inner_sides = shape((2 * rank, rows), F32), shape((2 * rank, 2 * rows), F32)
    unit = 2.0 * rows * rows * width
    pair_flops = 2.2 * unit

    both0, packed, ups0, s0, s1, h0, h1, inner0 = run(
        own_kernel,
        "own_rows",
        [consts, own, texts, twin, proj, down, up],
        [shape((rows, wide), BF16), shape((width, wide), BF16), shape((2 * rank, 2 * rows), BF16), sums, sums, narrow, narrow, inner_own],
        [pltpu.VMEM((rows, rows), BF16)],
        3.2 * unit + 2 * pair_flops,
    )
    ups0, across = tied(ups0, across)
    across_twin = from_ahead(across, "c", 1)
    square, block = pltpu.VMEM((rows, rows), BF16), shape((2 * rank, rows), BF16)

    def own_far(texts, inner):
        return run(
            own_far_kernel,
            "own_far",
            [consts, both0, texts, up, inner],
            [block, sums, narrow, inner_own],
            [square],
            pair_flops,
        )

    def side_far(texts, ups, inner, s, h):
        return run(
            side_far_kernel,
            "side_far",
            [consts, both1, texts, ups, inner, s, h],
            [sums, narrow, inner_sides],
            [pltpu.VMEM((rows, 2 * rows), BF16)],
            2 * pair_flops,
        )

    ups2, s2, h2, inner0 = own_far(across, inner0)
    inner0, ahead, behind, across_twin = tied(inner0, ahead, behind, across_twin)
    far = turned(ahead, 1)
    both1, h0, h1, inner1, w_near, w_twin = run(
        side_kernel,
        "side_rows",
        [consts, ahead, behind, texts, twin, ups0, packed, up, h0, h1],
        [shape((2 * rows, wide), BF16), narrow, narrow, inner_sides] + [shape((rows, 2 * rows), BF16)] * 2,
        [],
        6.4 * unit + 2 * pair_flops,
    )
    ups3, s3, h3, inner0 = own_far(across_twin, inner0)
    s3, h3, inner1 = side_far(across_twin, ups3, inner1, s3, h3)
    inner1, far = tied(inner1, far)
    far_twin = from_ahead(far, "c", 1)
    (far_both,) = run(embed_kernel, "embed_far", [far, packed, up], [shape((rows, wide), BF16)], [], 3.2 * unit, False)
    far_both_twin = from_ahead(far_both, "c", 1)
    s3 = from_ahead(s3, "c", 1)
    inner1, far_both = tied(inner1, far_both)
    s2, h2, inner1 = side_far(across, ups2, inner1, s2, h2)
    grad_down, grad_up = run(
        shares_kernel,
        "shares",
        [inner0, inner1, own, ahead, behind, h1, h3, twin, across_twin],
        [grads, grads],
        [],
        unit,
        False,
    )
    grad_up, far_twin, far_both_twin = tied(grad_up, far_twin, far_both_twin)
    kept, sent, both2, w0, w2 = run(
        last_kernel,
        "far_rows",
        [consts, far, far_twin, far_both, far_both_twin, texts, across, ups0, ups2, h0, h2, grad_down, grad_up],
        [grads, grads, shape((2 * rows, wide), BF16)] + [shape((rows, 2 * rows), BF16)] * 2,
        [],
        5 * unit,
    )

    def small(kernel, name, operands, outs, scratch=()):
        return run(kernel, name, operands, outs, scratch, 1, False)

    sizes = (272, 112)
    chunks = small(
        away_kernel, "away_sums", [w2, both2, s2, s3], [shape((n + (16 if k == 0 else 0), width), F32) for k, n in enumerate(sizes)]
    )
    chunks = [chunk.astype(F16) for chunk in chunks]

    def everyones(axis, order, other):
        def summed(block):
            others = [other(block, axis, d) for d in order]
            return small(sum_kernel, "sums", [block] + others, [quarter])[0]

        return summed

    def scattered(sent):
        pieces = small(quarter_kernel, "quarters", [kept, sent], [quarter] * 4, [pltpu.VMEM((rank, width), F32)])
        pieces = [pieces[0]] + [from_ahead(p, "z", d) for p, d in zip(pieces[1:], (1, 2, 3))]
        return small(sum_kernel, "sums", pieces, [quarter])[0]

    def gathered(block):
        pieces = [block] + [from_ahead(block, "z", d) for d in (2, 3, 1)]
        return small(functools.partial(place_kernel, float(rows * 16)), "places", pieces, [grads])[0]

    quarter = shape((rank // 4, width), F32)
    sent = from_ahead(sent, "c", 1)
    sent, *chunks = tied(sent, *chunks)
    total = scattered(sent)
    moved = from_ahead(chunks[0], "y", 1)
    (s1,) = small(twin_kernel, "twin_sums", [w_twin, both1, s1], [sums])
    total = everyones("x", (2, 3, 1), from_ahead)(total)
    total, c0, s1, chunk = tied(total, moved, s1, chunks[1])
    s1 = from_ahead(s1, "c", 1)
    total = everyones(("y", "h"), (1, 2, 3), from_ahead)(total)
    total, chunk, s1 = tied(total, chunk, s1)
    moved = from_ahead(chunk, "y", 1)
    total = gathered(total)
    (near,) = small(near_kernel, "near_sums", [w_near, both1, w0, both2, s0, s1], [sums])
    total, c1, near = tied(total, moved, near)
    other = from_ahead(total, "c", 1)
    (text_grad,) = small(finish_kernel, "finish", [near, c0.astype(F32), c1.astype(F32)], [sums])
    grad_down, grad_up = small(join_kernel, "joined", [total, other], [grads, grads])
    grad_down = grad_down.T
    return text_grad[None], grad_down, grad_up


def solution(mesh):
    grid = Mesh(mesh.devices.reshape(4, 2, 2, 2, 4), AXES)
    blk, dp = ("z", "y", "c"), ("h", "x")
    placed = (P(dp, blk, None), P(dp, blk, None), P(), P(), P(), P(), P())
    return jax.shard_map(
        shards,
        mesh=grid,
        in_specs=placed,
        out_specs=(P(dp, blk, None), P(), P()),
        check_vma=False,
    )
```

```python
import functools
import math

import jax
import jax.numpy as jnp
from jax import lax
from jax.experimental import pallas as pl
from jax.experimental.pallas import tpu as pltpu
from jax.sharding import Mesh, PartitionSpec as P

F32, BF16, F16 = jnp.float32, jnp.bfloat16, jnp.float16
AXES = ("z", "y", "c", "h", "x")
LOG2E = 1.4426950408889634
REACH = 14.0
MIB = 1 << 20


def tied(*values):
    return lax.optimization_barrier(values)


def from_ahead(block, axis, distance):
    n = lax.axis_size(axis)
    return lax.ppermute(block, axis, [((i + distance) % n, i) for i in range(n)])


def mm(a, b):
    return jnp.dot(a, b, preferred_element_type=F32)


def mm_nt(a, b):
    return lax.dot_general(a, b, (((1,), (1,)), ((), ())), preferred_element_type=F32)


def mm_tn(a, b):
    return lax.dot_general(a, b, (((0,), (0,)), ((), ())), preferred_element_type=F32)


def halves(a):
    high = a.astype(BF16)
    return high, (a - high.astype(F32)).astype(BF16)


def embed(images, at, both, packed, up):
    here = slice(at, at + images.shape[0])
    width, rank = up.shape[1], up.shape[0]
    products = mm(images[...], packed[...])
    hidden = products[:, width:].astype(BF16)
    both[here, :width] = (products[:, :width] + mm(hidden[:, :rank], up[...])).astype(BF16)
    both[here, width:] = hidden


def gate(sims, consts):
    power = jnp.minimum(sims * consts[0] + consts[1], 126.0)
    return (consts[2] / (1.0 + jnp.exp2(power))).astype(BF16)


def gate_matching(sims, consts):
    power = sims * consts[0] + consts[1]
    other = consts[2] / (1.0 + jnp.exp2(jnp.minimum(power, 126.0)))
    match = -consts[2] / (1.0 + jnp.exp2(jnp.minimum(-power, 126.0)))
    row = lax.broadcasted_iota(jnp.int32, sims.shape, 0)
    col = lax.broadcasted_iota(jnp.int32, sims.shape, 1)
    return jnp.where(row == col, match, other).astype(BF16)


def text_ups(texts, up, out, at):
    high, low = halves(mm_nt(up[...], texts[...]))
    out[:, at : at + texts.shape[0]] = jnp.concatenate([high, low])


def down_share(inner, images):
    rank = inner.shape[0] // 2
    pair = jnp.concatenate(halves(inner[:rank] + inner[rank:]))
    grad = mm(pair, images)
    return grad[:rank] + grad[rank:]


def up_share(hidden, texts, rank):
    pair = jnp.concatenate(halves(hidden[:, :rank]), axis=1)
    grad = mm_tn(pair, texts)
    return grad[:rank] + grad[rank:]


def consts_kernel(root, scale, offset, out):
    factor = scale[0] / root
    out[0] = -factor * LOG2E
    out[1] = -offset[0] * LOG2E
    out[2] = factor


def own_kernel(consts, own, t0, t1, proj, down, up, both, packed, ups, s0, s1, h0, h1, inner, w):
    width, rows, rank = proj.shape[1], own.shape[0], up.shape[0]
    packed[:, :width] = proj[...]
    packed[:, width : width + rank] = down[...].T
    packed[:, width + rank :] = jnp.zeros((packed.shape[0], packed.shape[1] - width - rank), BF16)
    embed(own, 0, both, packed, up)
    for k, (texts, s, h) in enumerate(((t0, s0, h0), (t1, s1, h1))):
        text_ups(texts, up, ups, k * rows)
        sims = mm_nt(texts[...], both[:, :width])
        w[...] = gate(sims, consts) if k else gate_matching(sims, consts)
        sums = mm(w[...], both[...])
        s[...], h[...] = sums[:, :width], sums[:, width:]
        part = mm(ups[:, k * rows : (k + 1) * rows], w[...])
        inner[...] = inner[...] + part if k else part


def side_kernel(consts, a, b, t0, t1, ups, packed, up, h0, h1, both, g0, g1, inner, w0, w1):
    width, rows = up.shape[1], a.shape[0]
    embed(a, 0, both, packed, up)
    embed(b, rows, both, packed, up)
    for k, (texts, h, g, w) in enumerate(((t0, h0, g0, w0), (t1, h1, g1, w1))):
        w[...] = gate(mm_nt(texts[...], both[:, :width]), consts)
        g[...] = h[...] + mm(w[...], both[:, width:])
        part = mm(ups[:, k * rows : (k + 1) * rows], w[...])
        inner[...] = inner[...] + part if k else part


def own_far_kernel(consts, both, texts, up, inner0, ups, s, h, inner, w):
    width = texts.shape[1]
    text_ups(texts, up, ups, 0)
    w[...] = gate(mm_nt(texts[...], both[:, :width]), consts)
    sums = mm(w[...], both[...])
    s[...], h[...] = sums[:, :width], sums[:, width:]
    inner[...] = inner0[...] + mm(ups[...], w[...])


def own_far_given_kernel(consts, both, texts, ups, inner0, s, h, inner, w):
    width = texts.shape[1]
    w[...] = gate(mm_nt(texts[...], both[:, :width]), consts)
    sums = mm(w[...], both[...])
    s[...], h[...] = sums[:, :width], sums[:, width:]
    inner[...] = inner0[...] + mm(ups[...], w[...])


def side_far_kernel(consts, both, texts, ups, inner0, s0, h0, s, h, inner, w):
    width = texts.shape[1]
    w[...] = gate(mm_nt(texts[...], both[:, :width]), consts)
    sums = mm(w[...], both[...])
    s[...], h[...] = s0[...] + sums[:, :width], h0[...] + sums[:, width:]
    inner[...] = inner0[...] + mm(ups[...], w[...])


def shares_kernel(inner0, inner1, own, a, b, h1, h3, t1, t3, grad_down, grad_up):
    rows, rank = own.shape[0], grad_up.shape[0]
    grad_up[...] = up_share(h1[...], t1[...], rank) + up_share(h3[...], t3[...], rank)
    grad_down[...] = (
        down_share(inner0[...], own[...])
        + down_share(inner1[:, :rows], a[...])
        + down_share(inner1[:, rows:], b[...])
    )


def embed_kernel(images, packed, up, both):
    embed(images, 0, both, packed, up)


def last_kernel(
    consts, x0, x1, e0, e1, t0, t1, ups0, ups1, h0, h1, grad_down, grad_up, kept, sent, both, w0, w1
):
    rows, width = t0.shape
    rank, blocks = grad_up.shape[0], (x0, x1)
    both[:rows], both[rows:] = e0[...], e1[...]
    inner, up_sum = None, grad_up[...]
    for texts, ups, h, w in ((t0, ups0, h0, w0), (t1, ups1, h1, w1)):
        w[...] = gate(mm_nt(texts[...], both[:, :width]), consts)
        up_sum = up_sum + up_share(h[...] + mm(w[...], both[:, width:]), texts[...], rank)
        part = mm(ups[:, :rows], w[...])
        inner = part if inner is None else inner + part
    down_sum, at = grad_down[...], 0
    for block in blocks:
        down_sum = down_sum + down_share(inner[:, at : at + block.shape[0]], block[...])
        at += block.shape[0]
    first = lax.axis_index("c") == 0
    kept[...] = jnp.where(first, down_sum, up_sum)
    sent[...] = jnp.where(first, up_sum, down_sum)


def twin_kernel(w, both, s, out):
    out[...] = s[...] + mm(w[...], both[:, : s.shape[1]])


def near_kernel(w0, both0, w1, both1, s, twin, out):
    width = s.shape[1]
    out[...] = s[...] + twin[...] + mm(w0[...], both0[:, :width]) + mm(w1[...], both1[:, :width])


def away_kernel(w, both, s, twin, *outs):
    rows, width = s.shape
    value = s[...] + twin[...] + mm(w[...], both[:, :width])
    top = jnp.maximum(jnp.max(jnp.abs(value), keepdims=True), 1e-30)
    power = jnp.ceil(jnp.log2(top))
    value = value * jnp.exp2(REACH - power)
    tail, at = outs[0].shape[0] - 16, 0
    for k, out in enumerate(outs):
        part = out.shape[0] if k else tail
        out[:part] = value[at : at + part]
        at += part
    outs[0][tail:] = jnp.broadcast_to(power, (16, width))


def finish_kernel(near, c0, c1, out):
    tail, at = c0.shape[0] - 16, 0
    scale = jnp.exp2(c0[tail : tail + 1, :] - REACH)
    for k, chunk in enumerate((c0, c1)):
        part = chunk.shape[0] if k else tail
        out[at : at + part] = near[at : at + part] + chunk[:part] * scale
        at += part


def quarter_kernel(a, b, o0, o1, o2, o3, total):
    total[...] = a[...] + b[...]
    here, part = lax.axis_index("z"), o0.shape[0]
    for out, d in ((o0, 0), (o1, 1), (o2, 2), (o3, 3)):
        out[...] = total[pl.ds(pl.multiple_of(((here + 4 - d) % 4) * part, part), part), :]


def sum_kernel(a, b, c, d, out):
    out[...] = a[...] + b[...] + c[...] + d[...]


def place_kernel(pairs, a, b, c, d, out):
    here, part = lax.axis_index("z"), a.shape[0]
    for block, k in ((a, 0), (b, 2), (c, 3), (d, 1)):
        out[pl.ds(pl.multiple_of(((here + k) % 4) * part, part), part), :] = block[...] / pairs


def join_kernel(a, b, down, up):
    first = lax.axis_index("c") == 0
    down[...] = jnp.where(first, a[...], b[...])
    up[...] = jnp.where(first, b[...], a[...])


def run(kernel, name, operands, outs, scratch, flops, consts=True):
    spec = pl.BlockSpec(memory_space=pltpu.VMEM)
    ins = [spec] * len(operands)
    if consts:
        ins[0] = pl.BlockSpec(memory_space=pltpu.SMEM)
    size = sum(math.prod(o.shape) * o.dtype.itemsize for o in list(operands) + list(outs))
    return pl.pallas_call(
        kernel,
        in_specs=ins,
        out_specs=[spec] * len(outs),
        out_shape=outs,
        scratch_shapes=scratch,
        compiler_params=pltpu.CompilerParams(vmem_limit_bytes=16 * MIB),
        cost_estimate=pl.CostEstimate(flops=int(flops), bytes_accessed=size, transcendentals=0),
        name=name,
    )(*operands)


def shards(images, texts, proj, down, up, scale, offset):
    own, texts = images[0], texts[0]
    rows, width = texts.shape
    rank = down.shape[1]
    wide = width + 128
    scalar = pl.BlockSpec(memory_space=pltpu.SMEM)
    consts = pl.pallas_call(
        functools.partial(consts_kernel, math.sqrt(width)),
        in_specs=[scalar, scalar],
        out_specs=scalar,
        out_shape=jax.ShapeDtypeStruct((3,), F32),
        compiler_params=pltpu.CompilerParams(vmem_limit_bytes=MIB),
        name="consts",
    )(scale, offset)
    down = down.T

    def turned(block, way):
        n = lax.axis_size("z")
        step = lambda z, c: (z + (way if c == 0 else -way)) % n
        return lax.ppermute(block, ("z", "c"), [(2 * step(z, c) + c, 2 * z + c) for z in range(n) for c in range(2)])

    ahead = turned(own, 1)
    behind = turned(own, -1)
    across = from_ahead(texts, "y", 1)
    twin = from_ahead(texts, "c", 1)

    shape = jax.ShapeDtypeStruct
    sums, narrow, grads = shape((rows, width), F32), shape((rows, 128), F32), shape((rank, width), F32)
    inner_own, inner_sides = shape((2 * rank, rows), F32), shape((2 * rank, 2 * rows), F32)
    unit = 2.0 * rows * rows * width
    pair_flops = 2.2 * unit

    both0, packed, ups0, s0, s1, h0, h1, inner0 = run(
        own_kernel,
        "own_rows",
        [consts, own, texts, twin, proj, down, up],
        [shape((rows, wide), BF16), shape((width, wide), BF16), shape((2 * rank, 2 * rows), BF16), sums, sums, narrow, narrow, inner_own],
        [pltpu.VMEM((rows, rows), BF16)],
        3.2 * unit + 2 * pair_flops,
    )
    ups0, across = tied(ups0, across)
    across_twin = from_ahead(across, "c", 1)
    square, block = pltpu.VMEM((rows, rows), BF16), shape((2 * rank, rows), BF16)

    def own_far(texts, inner):
        return run(
            own_far_kernel,
            "own_far",
            [consts, both0, texts, up, inner],
            [block, sums, narrow, inner_own],
            [square],
            pair_flops,
        )

    def side_far(texts, ups, inner, s, h):
        return run(
            side_far_kernel,
            "side_far",
            [consts, both1, texts, ups, inner, s, h],
            [sums, narrow, inner_sides],
            [pltpu.VMEM((rows, 2 * rows), BF16)],
            2 * pair_flops,
        )

    ups2, s2, h2, inner0 = own_far(across, inner0)
    ups3 = from_ahead(ups2, "c", 1)
    inner0, ahead, behind, across_twin = tied(inner0, ahead, behind, across_twin)
    far = turned(ahead, 1)
    both1, h0, h1, inner1, w_near, w_twin = run(
        side_kernel,
        "side_rows",
        [consts, ahead, behind, texts, twin, ups0, packed, up, h0, h1],
        [shape((2 * rows, wide), BF16), narrow, narrow, inner_sides] + [shape((rows, 2 * rows), BF16)] * 2,
        [],
        6.4 * unit + 2 * pair_flops,
    )
    s3, h3, inner0 = run(
        own_far_given_kernel,
        "own_far",
        [consts, both0, across_twin, ups3, inner0],
        [sums, narrow, inner_own],
        [square],
        pair_flops,
    )
    s3, h3, inner1 = side_far(across_twin, ups3, inner1, s3, h3)
    inner1, far = tied(inner1, far)
    far_twin = from_ahead(far, "c", 1)
    (far_both,) = run(embed_kernel, "embed_far", [far, packed, up], [shape((rows, wide), BF16)], [], 3.2 * unit, False)
    far_both_twin = from_ahead(far_both, "c", 1)
    s3 = from_ahead(s3, "c", 1)
    inner1, far_both = tied(inner1, far_both)
    s2, h2, inner1 = side_far(across, ups2, inner1, s2, h2)
    grad_down, grad_up = run(
        shares_kernel,
        "shares",
        [inner0, inner1, own, ahead, behind, h1, h3, twin, across_twin],
        [grads, grads],
        [],
        unit,
        False,
    )
    grad_up, far_twin, far_both_twin = tied(grad_up, far_twin, far_both_twin)
    kept, sent, both2, w0, w2 = run(
        last_kernel,
        "far_rows",
        [consts, far, far_twin, far_both, far_both_twin, texts, across, ups0, ups2, h0, h2, grad_down, grad_up],
        [grads, grads, shape((2 * rows, wide), BF16)] + [shape((rows, 2 * rows), BF16)] * 2,
        [],
        5 * unit,
    )

    def small(kernel, name, operands, outs, scratch=()):
        return run(kernel, name, operands, outs, scratch, 1, False)

    sizes = (272, 112)
    chunks = small(
        away_kernel, "away_sums", [w2, both2, s2, s3], [shape((n + (16 if k == 0 else 0), width), F32) for k, n in enumerate(sizes)]
    )
    chunks = [chunk.astype(F16) for chunk in chunks]

    def everyones(axis, order, other):
        def summed(block):
            others = [other(block, axis, d) for d in order]
            return small(sum_kernel, "sums", [block] + others, [quarter])[0]

        return summed

    def scattered(sent):
        pieces = small(quarter_kernel, "quarters", [kept, sent], [quarter] * 4, [pltpu.VMEM((rank, width), F32)])
        pieces = [pieces[0]] + [from_ahead(p, "z", d) for p, d in zip(pieces[1:], (1, 2, 3))]
        return small(sum_kernel, "sums", pieces, [quarter])[0]

    def gathered(block):
        pieces = [block] + [from_ahead(block, "z", d) for d in (2, 3, 1)]
        return small(functools.partial(place_kernel, float(rows * 16)), "places", pieces, [grads])[0]

    quarter = shape((rank // 4, width), F32)
    sent = from_ahead(sent, "c", 1)
    sent, *chunks = tied(sent, *chunks)
    total = scattered(sent)
    moved = from_ahead(chunks[0], "y", 1)
    (s1,) = small(twin_kernel, "twin_sums", [w_twin, both1, s1], [sums])
    total = everyones("x", (2, 3, 1), from_ahead)(total)
    total, c0, s1, chunk = tied(total, moved, s1, chunks[1])
    s1 = from_ahead(s1, "c", 1)
    total = everyones(("y", "h"), (1, 2, 3), from_ahead)(total)
    total, chunk, s1 = tied(total, chunk, s1)
    moved = from_ahead(chunk, "y", 1)
    total = gathered(total)
    (near,) = small(near_kernel, "near_sums", [w_near, both1, w0, both2, s0, s1], [sums])
    total, c1, near = tied(total, moved, near)
    other = from_ahead(total, "c", 1)
    (text_grad,) = small(finish_kernel, "finish", [near, c0.astype(F32), c1.astype(F32)], [sums])
    grad_down, grad_up = small(join_kernel, "joined", [total, other], [grads, grads])
    grad_down = grad_down.T
    return text_grad[None], grad_down, grad_up


def solution(mesh):
    grid = Mesh(mesh.devices.reshape(4, 2, 2, 2, 4), AXES)
    blk, dp = ("z", "y", "c"), ("h", "x")
    placed = (P(dp, blk, None), P(dp, blk, None), P(), P(), P(), P(), P())
    return jax.shard_map(
        shards,
        mesh=grid,
        in_specs=placed,
        out_specs=(P(dp, blk, None), P(), P()),
        check_vma=False,
    )
```
